512 devices in a mesh: dp: 4 (over x_hi, core), ctx: 128 (over z, x_lo, y).
Axes of the slice: x: 4 (x_hi: 2, x_lo: 2; x = x_hi * 2 + x_lo), y: 8, z: 8, core: 2. Of those that a mesh axis runs over, the one named last changes fastest.
Arguments:
- out_grad: bfloat16 [262144, 4608], P(('dp', 'ctx')), may hold values from -1 to 1
- adapter_inner: bfloat16 [262144, 16], P(('dp', 'ctx')), may hold values from -32 to 32
- doc_lengths: int32 [4, 64], P('dp'), may hold values from 1 to 1536, 65536 in all within a row
- slab_offset: int32 [4], P('dp'), may hold values from 1 to 1535
- included: int32 [4, 64], P('dp'), may hold values 0 or 1
Outputs:
- adapter_second_gradient: float32 [4608, 16], P(('dp', 'ctx'))
- doc_norms: float32 [4, 64], P('dp')
The draws below stay inside these ranges and needn't reach their ends.
Inputs may be any that keep to these rules, and one draw needn't show every extreme that they name: `doc_lengths`: in each row the lengths sum to 65536, and the largest is exactly 1536.
All inputs are finite; a program needn't handle non-finite values. No bound on the sum of `included` on one device may be relied on, other than what follows from the above.
Results may differ from the reference program's by a relative error of at most 0.0022.
Values may be sent and summed in bfloat16 or wider, within the bound.
A program may use at most 64 MiB of HBM per device.

```python
import math
import jax
import jax.numpy as jnp
import numpy as np
from jax import lax

D = 4608
RANK = 16
CB = 512
LMAX = 1536
BATCHES = 4
NDOC = 64
TOKB = 65536
TOKENS = 262144
N_CTX = 128


def common_part(key, row_count, col_count):
    anchor_count = row_count // CB + 1
    anchors = jax.random.normal(key, (anchor_count, col_count), jnp.float32)
    positions = jnp.arange(row_count)
    lower_node = positions // CB
    fraction = (positions % CB).astype(jnp.float32) / CB
    return anchors[lower_node] * (1.0 - fraction)[:, None] + anchors[lower_node + 1] * fraction[:, None]


def noisy_rows(key, row_count, col_count):
    subkeys = jax.random.split(key, 2)
    noise_part = jax.random.truncated_normal(subkeys[0], -4.0, 4.0, (row_count, col_count), jnp.float32)
    common = common_part(subkeys[1], row_count, col_count)
    return noise_part + CB ** (-0.25) * common


def draw_adapter_inner(key, part):
    values = noisy_rows(jax.random.fold_in(key, 11), TOKENS, RANK)
    return jnp.clip(values, -32.0, 32.0).astype(jnp.bfloat16)


def draw_out_grad(key, part):
    values = noisy_rows(jax.random.fold_in(key, 23), TOKENS, D) * D ** (-0.5)
    return jnp.clip(values, -1.0, 1.0).astype(jnp.bfloat16)


def with_ends(values, key, low, top_value):
    longest = values.shape.index(max(values.shape))
    spots = []
    for shift in (0, 1):
        where = [jax.random.randint(jax.random.fold_in(key, axis), (), 0, length) for axis, length in enumerate(values.shape)]
        where[longest] = (where[longest] + shift) % values.shape[longest]
        spots.append(tuple(where))
    return values.at[spots[0]].set(low).at[spots[1]].set(top_value)


def profile(amount, total, bound, skew):
    portions = [(1 << 20) // math.isqrt(standing ** skew) + 1 for standing in range(2, amount + 1)]
    rest, given = total - bound - (amount - 1), [1] * (amount - 1)
    while rest > 0:
        candidates = [i for i in range(amount - 1) if given[i] < bound]
        mass, remaining = sum([portions[i] for i in candidates]), rest
        for i in candidates:
            more = min(bound - given[i], max(1, remaining * portions[i] // mass), rest)
            given[i] = given[i] + more
            rest = rest - more
    return np.array([bound] + given)


def uneven_parts(own_key, number_of, total, bound, slope):
    if number_of == 2:
        one = jax.random.randint(own_key, (), max(1, total - bound), min(bound, total - 1) + 1)
        return jnp.stack([one, total - one])
    sizes = jnp.asarray(profile(number_of, total, bound, slope), jnp.int32)
    couples = (number_of - 1) // 2
    donor, sink = sizes[1:1 + 2 * couples:2], sizes[2:2 + 2 * couples:2]
    slack = jnp.minimum(donor - 1, bound - sink)
    moved = jax.random.randint(jax.random.fold_in(own_key, 1), (couples,), 0, 1 << 20) % (slack + 1)
    sizes = sizes.at[1:1 + 2 * couples:2].set(donor - moved).at[2:2 + 2 * couples:2].set(sink + moved)
    return sizes[jax.random.permutation(jax.random.fold_in(own_key, 2), number_of)]


def setup_inputs(seed: int = 0) -> dict:
    keys = jax.random.split(jax.random.key(seed), 6)
    out_grad = draw_out_grad(jax.random.fold_in(keys[5], 71), 0)
    adapter_inner = draw_adapter_inner(jax.random.fold_in(keys[5], 71), 0)
    doc_lengths = jax.vmap(lambda own: uneven_parts(own, NDOC, TOKB, LMAX, 1))(jax.random.split(keys[2], BATCHES)).reshape((BATCHES, NDOC)).astype(jnp.int32)
    slab_offset = with_ends(jax.random.randint(keys[3], (BATCHES,), 1, LMAX), jax.random.fold_in(keys[3], 1), 1, LMAX - 1).astype(jnp.int32)
    included = with_ends((jax.random.randint(keys[4], (BATCHES, NDOC), 0, 2) < 1).astype(jnp.int32), jax.random.fold_in(keys[4], 1), 0, 1)
    return dict(out_grad=out_grad, adapter_inner=adapter_inner, doc_lengths=doc_lengths, slab_offset=slab_offset, included=included)


clip_norm = 128.0

def document_ids(lengths, offset, positions):
    doc_ends = jnp.cumsum(lengths).astype(jnp.int32)
    starts = (doc_ends - lengths).astype(jnp.int32)
    longest = jnp.argmax(lengths).astype(jnp.int32)
    labels = jnp.arange(lengths.shape[0], dtype=jnp.int32)
    doc_shift = jnp.sum(jnp.where(labels == longest, starts, 0)).astype(jnp.int32) + offset
    packed = (positions + doc_shift) % (N_CTX * CB)
    return lax.optimization_barrier(jnp.sum((doc_ends[None, :] <= packed[:, None]).astype(jnp.int32), axis=1)).astype(jnp.int32)

def per_document(inner_rows, grad_rows, doc_ids):
    inner_blocks = inner_rows.reshape(N_CTX, CB, RANK)
    grad_blocks = grad_rows.reshape(N_CTX, CB, D)
    id_blocks = doc_ids.reshape(N_CTX, CB)
    labels = jnp.arange(NDOC, dtype=jnp.int32)

    def add_block(accumulated, block_items):
        inner_block, grad_block, id_block = block_items
        member = (id_block[:, None] == labels[None, :]).astype(jnp.float32)
        spread = (member[:, :, None] * inner_block.astype(jnp.float32)[:, None, :]).reshape(CB, NDOC * RANK)
        return (accumulated + jnp.dot(spread.T, grad_block.astype(jnp.float32), precision=lax.Precision.HIGHEST), None)
    result, unused = lax.scan(add_block, jnp.zeros((NDOC * RANK, D), jnp.float32), (inner_blocks, grad_blocks, id_blocks))
    return result

def reference(out_grad, adapter_inner, doc_lengths, slab_offset, included):
    tokens_batch = N_CTX * CB
    total_grad = jnp.zeros((D, RANK), jnp.float32)
    row_norm_values = []
    for batch_index in range(BATCHES):
        first_row = batch_index * tokens_batch
        inner_rows = adapter_inner[first_row:first_row + tokens_batch]
        grad_rows = out_grad[first_row:first_row + tokens_batch]
        doc_ids = document_ids(doc_lengths[batch_index], slab_offset[batch_index], jnp.arange(tokens_batch, dtype=jnp.int32))
        document_gradient_rows = per_document(inner_rows, grad_rows, doc_ids)
        document_grad_norm = jnp.sqrt(lax.optimization_barrier(jnp.sum(document_gradient_rows.reshape(NDOC, RANK * D) ** 2, axis=1)))
        clip_factor = included[batch_index].astype(jnp.float32) * clip_norm / jnp.maximum(document_grad_norm, clip_norm)
        scaled = (clip_factor[doc_ids][:, None] * inner_rows.astype(jnp.float32)).astype(jnp.bfloat16)
        total_grad = total_grad + jnp.dot(grad_rows.T, scaled, preferred_element_type=jnp.float32)
        row_norm_values.append(document_grad_norm)
    return (total_grad, jnp.stack(row_norm_values))
```

```python
import functools

import jax
import jax.numpy as jnp
from jax import lax
from jax.experimental import pallas as pl
from jax.experimental.pallas import tpu as pltpu
from jax.sharding import PartitionSpec as P

CLIP_NORM = 128.0
LONGEST = 1536.0
LOCAL_DOCS = 23
REACH = 3
PARTS = 4
MESH = pl.DeviceIdType.MESH
F32 = jnp.float32
BF16 = jnp.bfloat16


def lane_tiles(array):
    return [array[:, k : k + 128] for k in range(0, array.shape[1], 128)]


def kernel(
    geometry, grad_hbm, inner_ref, len_ref, off_ref, inc_ref,
    out_ref, norm_ref,
    grad, lhs, last_out, first_out, last_in, first_in, last_far, first_far,
    terms_out, terms_in, clipped, send_1, recv_1, send_2, recv_2, send_3, recv_3,
    load_sem, halo_send, halo_recv, terms_send, terms_recv,
    send_sem_1, recv_sem_1, send_sem_2, recv_sem_2, send_sem_3, recv_sem_3,
):
    n_dp, n_z, n_x, n_y = geometry
    n_ctx = n_z * n_x * n_y
    rows, width = grad.shape
    rank = inner_ref.shape[0]
    docs = len_ref.shape[1]
    part = width // PARTS
    tokens = n_ctx * rows
    dp = lax.axis_index("dp")
    block = lax.axis_index("ctx")
    z, x, y = block // (n_x * n_y), (block // n_y) % n_x, block % n_y
    n_group = n_dp * n_x
    group = dp * n_x + x

    def along(distance):
        return (dp, lax.rem(block + distance + n_ctx, n_ctx))

    def in_group(g):
        return (g // n_x, z * (n_x * n_y) + lax.rem(g, n_x) * n_y + y)

    def in_z(other):
        return (dp, other * (n_x * n_y) + x * n_y + y)

    def in_y(other):
        return (dp, z * (n_x * n_y) + x * n_y + other)

    loads = []
    for p in range(PARTS):
        columns = pl.ds(p * part, part)
        loads.append(
            pltpu.make_async_copy(grad_hbm.at[:, columns], grad.at[:, columns], load_sem.at[p])
        )
        loads[-1].start()

    barrier = pltpu.get_barrier_semaphore()
    greeted = 0
    for distance in range(1, REACH + 1):
        for sign in (1, -1):
            pl.semaphore_signal(
                barrier, inc=1, device_id=along(sign * distance), device_id_type=MESH
            )
            greeted += 1
    for size, me, where in ((n_group, group, in_group), (n_z, z, in_z), (n_y, y, in_y)):
        for step in range(1, size):
            pl.semaphore_signal(
                barrier, inc=1, device_id=where(lax.rem(me + step, size)), device_id_type=MESH
            )
            greeted += 1

    lengths = len_ref[...].astype(F32)
    down = lax.broadcasted_iota(jnp.int32, (docs, docs), 0)
    across = lax.broadcasted_iota(jnp.int32, (docs, docs), 1)
    own = down == across
    spread = jnp.broadcast_to(lengths, (docs, docs))
    ends = jnp.sum(jnp.where(across <= down, spread, 0.0), axis=1, keepdims=True)
    length = jnp.sum(jnp.where(own, spread, 0.0), axis=1, keepdims=True)
    start = jnp.min(
        jnp.where(length == LONGEST, ends - length, float(tokens)), axis=0, keepdims=True
    )
    shift = start + off_ref[0].astype(F32)

    def ids_of(positions):
        packed = positions.astype(F32) + shift
        packed = jnp.where(packed >= tokens, packed - tokens, packed)
        return jnp.sum(jnp.where(ends <= packed, 1.0, 0.0), axis=0, keepdims=True)

    ids = ids_of(block * rows + lax.broadcasted_iota(jnp.int32, (1, rows), 1))
    lane = lax.broadcasted_iota(jnp.int32, (1, 128), 1)
    places = jnp.zeros((1, 128), jnp.int32)
    offsets = (-rows - 1, -1, 0, rows, 2 * rows, rows - 1)
    for i, offset in enumerate(offsets):
        places = jnp.where(lane == i, offset, places)
    places = places + block * rows
    places = jnp.where(places < 0, places + tokens, places)
    places = jnp.where(places >= tokens, places - tokens, places)
    edge_ids = ids_of(places)
    behind_2, behind_1, first, ahead_1, ahead_2, last = [
        jnp.sum(jnp.where(lane == i, edge_ids, 0.0), axis=1, keepdims=True)
        for i in range(len(offsets))
    ]

    inner = inner_ref[...].astype(F32)
    local = ids - first
    local = jnp.where(local < 0.0, local + docs, local)
    lhs[0:rank, :] = jnp.where(ids == last, inner, 0.0).astype(BF16)
    for q in range(LOCAL_DOCS):
        lhs[(q + 1) * rank : (q + 2) * rank, :] = jnp.where(local == float(q), inner, 0.0).astype(
            BF16
        )

    def halo(p):
        columns = pl.ds(p * part, part)
        far = pl.ds((p % (PARTS // 2)) * part, part)
        low = p < PARTS // 2
        moves = [
            (last_out.at[:, columns], last_in.at[:, columns], along(1)),
            (first_out.at[:, columns], first_in.at[:, columns], along(-1)),
            (last_out.at[:, columns], last_far.at[:, far], along(2))
            if low
            else (first_out.at[:, columns], first_far.at[:, far], along(-2)),
        ]
        return [
            pltpu.make_async_remote_copy(
                src_ref=src,
                dst_ref=dst,
                send_sem=halo_send.at[p, i],
                recv_sem=halo_recv.at[p, i],
                device_id=to,
                device_id_type=MESH,
            )
            for i, (src, dst, to) in enumerate(moves)
        ]

    doc_rows = LOCAL_DOCS * rank
    squares = jnp.zeros((doc_rows, 128), F32)
    halos = []
    for p in range(PARTS):
        loads[p].wait()
        columns = slice(p * part, (p + 1) * part)
        sums = jnp.dot(lhs[...], grad[:, columns], preferred_element_type=F32)
        last_out[:, columns] = sums[0:rank].astype(BF16)
        first_out[:, columns] = sums[rank : 2 * rank].astype(BF16)
        if p == 0:
            pl.semaphore_wait(barrier, greeted)
        halos.append(halo(p))
        for copy in halos[-1]:
            copy.start()
        for tile in lane_tiles(sums[rank:]):
            squares = squares + tile * tile

    by_row = jnp.sum(squares, axis=1, keepdims=True)
    label = first + lax.shift_right_logical(
        lax.broadcasted_iota(jnp.int32, (doc_rows, 1), 0), rank.bit_length() - 1
    ).astype(F32)
    label = jnp.where(label >= docs, label - docs, label)
    lane_f = lane.astype(F32)
    terms = jnp.sum(jnp.where(label == lane_f, by_row, 0.0), axis=0, keepdims=True)

    def flag(condition):
        return jnp.where(condition, 2.0, 0.0)

    pair_1 = flag(behind_1 == first)
    pair_2 = flag(behind_1 == ahead_1)
    pair_3_ahead = flag(behind_1 == ahead_2)
    pair_3_behind = flag(behind_2 == ahead_1)
    crossed = jnp.zeros((rank, 128), F32)
    for p in range(PARTS):
        columns = slice(p * part, (p + 1) * part)
        far = slice((p % (PARTS // 2)) * part, (p % (PARTS // 2) + 1) * part)
        for copy in halos[p]:
            copy.wait_recv()
        from_behind = last_in[:, columns].astype(F32)
        from_ahead = first_in[:, columns].astype(F32)
        partner = pair_1 * first_out[:, columns].astype(F32) + pair_2 * from_ahead
        if p < PARTS // 2:
            product = from_behind * partner + (pair_3_behind * from_ahead) * last_far[
                :, far
            ].astype(F32)
        else:
            product = from_behind * (partner + pair_3_ahead * first_far[:, far].astype(F32))
        for tile in lane_tiles(product):
            crossed = crossed + tile
    cross = jnp.sum(jnp.sum(crossed, axis=1, keepdims=True), axis=0, keepdims=True)
    terms = terms + jnp.where(lane_f == first, cross, 0.0)

    terms_out[...] = jnp.broadcast_to(terms, (8, 128))
    news = []
    for distance in range(1, REACH + 1):
        for sign in (1, -1):
            slot = len(news)
            news.append(
                pltpu.make_async_remote_copy(
                    src_ref=terms_out,
                    dst_ref=terms_in.at[slot],
                    send_sem=terms_send.at[slot],
                    recv_sem=terms_recv.at[slot],
                    device_id=along(sign * distance),
                    device_id_type=MESH,
                )
            )
            news[-1].start()
    near = terms
    for slot, copy in enumerate(news):
        copy.wait_recv()
        near = near + terms_in[slot, 0:1, :]

    norms = jnp.sqrt(jnp.maximum(near[:, 0:docs], 0.0))
    factor = inc_ref[...].astype(F32) * CLIP_NORM / jnp.maximum(norms, CLIP_NORM)
    factor = jnp.sum(jnp.where(own, jnp.broadcast_to(factor, (docs, docs)), 0.0), axis=1, keepdims=True)
    name = lax.broadcasted_iota(jnp.int32, (docs, 1), 0).astype(F32)
    token_factor = jnp.sum(jnp.where(ids == name, factor, 0.0), axis=0, keepdims=True)
    scaled = (token_factor * inner).astype(BF16)
    for p in range(PARTS):
        columns = slice(p * part, (p + 1) * part)
        clipped[:, columns] = jnp.dot(scaled, grad[:, columns], preferred_element_type=F32)

    each = width // (n_dp * n_ctx)
    run = n_y * each
    half = n_z * run
    for g in range(n_group):
        base = (g // n_x) * (n_ctx * each) + (g % n_x) * run
        for k in range(n_z):
            column = base + k * (n_x * run)
            send_1[g, :, k * run : (k + 1) * run] = clipped[0:8, column : column + run]
            send_1[g, :, half + k * run : half + (k + 1) * run] = clipped[8:16, column : column + run]
        send_1[g, :, 2 * half : 2 * half + 128] = jnp.broadcast_to(terms, (8, 128))

    def exchange(size, me, where, out, into, out_sem, in_sem):
        copies = []
        for step in range(1, size):
            to = lax.rem(me + step, size)
            copies.append(
                pltpu.make_async_remote_copy(
                    src_ref=out.at[to],
                    dst_ref=into.at[me],
                    send_sem=out_sem.at[step],
                    recv_sem=in_sem.at[me],
                    device_id=where(to),
                    device_id_type=MESH,
                )
            )
            copies[-1].start()
        into[me] = out[me]
        for step in range(1, size):
            source = lax.rem(me + size - step, size)
            pltpu.make_async_remote_copy(
                src_ref=out.at[source],
                dst_ref=into.at[source],
                send_sem=out_sem.at[step],
                recv_sem=in_sem.at[source],
                device_id=where(source),
                device_id_type=MESH,
            ).wait_recv()
        return copies

    sent = exchange(n_group, group, in_group, send_1, recv_1, send_sem_1, recv_sem_1)
    total = recv_1[0, :, 0 : 2 * half]
    for g in range(1, n_group):
        total = total + recv_1[g, :, 0 : 2 * half]
    all_terms = recv_1[dp * n_x, :, 2 * half : 2 * half + 128]
    for k in range(1, n_x):
        all_terms = all_terms + recv_1[dp * n_x + k, :, 2 * half : 2 * half + 128]
    for k in range(n_z):
        send_2[k, 0:8, 0:run] = total[:, k * run : (k + 1) * run]
        send_2[k, 8:16, 0:run] = total[:, half + k * run : half + (k + 1) * run]
        send_2[k, 16:24, :] = all_terms
    sent += exchange(n_z, z, in_z, send_2, recv_2, send_sem_2, recv_sem_2)
    total = recv_2[0, 0:16, 0:run]
    all_terms = recv_2[0, 16:24, :]
    for k in range(1, n_z):
        total = total + recv_2[k, 0:16, 0:run]
        all_terms = all_terms + recv_2[k, 16:24, :]
    for k in range(n_y):
        send_3[k, 0:16, 0:each] = total[:, k * each : (k + 1) * each]
        send_3[k, 16:24, :] = all_terms
    sent += exchange(n_y, y, in_y, send_3, recv_3, send_sem_3, recv_sem_3)
    total = recv_3[0, 0:16, 0:each]
    all_terms = recv_3[0, 16:17, 0:docs]
    for k in range(1, n_y):
        total = total + recv_3[k, 0:16, 0:each]
        all_terms = all_terms + recv_3[k, 16:17, 0:docs]
    out_ref[...] = total
    norm_ref[...] = jnp.sqrt(jnp.maximum(all_terms, 0.0))

    for copies in halos:
        for copy in copies:
            copy.wait_send()
    for copy in news + sent:
        copy.wait_send()


def on_device(geometry, out_grad, adapter_inner, doc_lengths, slab_offset, included):
    n_dp, n_z, n_x, n_y = geometry
    n_group = n_dp * n_x
    rows, width = out_grad.shape
    rank = adapter_inner.shape[1]
    docs = doc_lengths.shape[1]
    each = width // (n_dp * n_z * n_x * n_y)
    depth = (LOCAL_DOCS + 1) * rank
    long = 2 * n_z * n_y * each + 128
    in_vmem = pl.BlockSpec(memory_space=pltpu.VMEM)
    dma = pltpu.SemaphoreType.DMA
    gradient, norms = pl.pallas_call(
        functools.partial(kernel, geometry),
        out_shape=(
            jax.ShapeDtypeStruct((rank, each), F32),
            jax.ShapeDtypeStruct((1, docs), F32),
        ),
        in_specs=[
            pl.BlockSpec(memory_space=pl.ANY),
            in_vmem,
            in_vmem,
            pl.BlockSpec(memory_space=pltpu.SMEM),
            in_vmem,
        ],
        out_specs=(in_vmem, in_vmem),
        scratch_shapes=[
            pltpu.VMEM((rows, width), BF16),
            pltpu.VMEM((depth, rows), BF16),
            pltpu.VMEM((rank, width), BF16),
            pltpu.VMEM((rank, width), BF16),
            pltpu.VMEM((rank, width), BF16),
            pltpu.VMEM((rank, width), BF16),
            pltpu.VMEM((rank, width // 2), BF16),
            pltpu.VMEM((rank, width // 2), BF16),
            pltpu.VMEM((8, 128), F32),
            pltpu.VMEM((2 * REACH, 8, 128), F32),
            pltpu.VMEM((rank, width), F32),
            pltpu.VMEM((n_group, 8, long), F32),
            pltpu.VMEM((n_group, 8, long), F32),
            pltpu.VMEM((n_z, 24, 128), F32),
            pltpu.VMEM((n_z, 24, 128), F32),
            pltpu.VMEM((n_y, 24, 128), F32),
            pltpu.VMEM((n_y, 24, 128), F32),
            dma((PARTS,)),
            dma((PARTS, 3)),
            dma((PARTS, 3)),
            dma((2 * REACH,)),
            dma((2 * REACH,)),
            dma((n_group,)),
            dma((n_group,)),
            dma((n_z,)),
            dma((n_z,)),
            dma((n_y,)),
            dma((n_y,)),
        ],
        compiler_params=pltpu.CompilerParams(
            collective_id=0, has_side_effects=True, vmem_limit_bytes=40 * 2**20
        ),
    )(out_grad, adapter_inner.T, doc_lengths, slab_offset, included)
    return gradient.T, norms


def solution(mesh):
    n_x, n_y = 2, 8
    geometry = (mesh.shape["dp"], mesh.shape["ctx"] // (n_x * n_y), n_x, n_y)
    placed = (P(("dp", "ctx"), None), P(("dp", "ctx"), None), P("dp", None), P("dp"), P("dp", None))
    return jax.shard_map(
        functools.partial(on_device, geometry),
        mesh=mesh,
        in_specs=placed,
        out_specs=(P(("dp", "ctx"), None), P("dp", None)),
        check_vma=False,
    )
```

```python
import functools

import jax
import jax.numpy as jnp
from jax import lax
from jax.experimental import pallas as pl
from jax.experimental.pallas import tpu as pltpu
from jax.sharding import PartitionSpec as P

CLIP_NORM = 128.0
LONGEST = 1536.0
LOCAL_DOCS = 23
REACH = 3
PARTS = 4
MESH = pl.DeviceIdType.MESH
F32 = jnp.float32
BF16 = jnp.bfloat16


def lane_tiles(array):
    return [array[:, k : k + 128] for k in range(0, array.shape[1], 128)]


def kernel(
    geometry, grad_hbm, inner_hbm, len_hbm, off_ref, inc_hbm,
    out_ref, norm_ref,
    grad, inner_ref, len_ref, inc_ref, lhs, last_out, first_out, last_in, first_in, last_far, first_far,
    terms_out, terms_in, clipped, send_1, recv_1, send_2, recv_2, send_3, recv_3,
    load_sem, small_sem, halo_send, halo_recv, terms_send, terms_recv,
    send_sem_1, recv_sem_1, send_sem_2, recv_sem_2, send_sem_3, recv_sem_3,
):
    n_dp, n_z, n_x, n_y = geometry
    n_ctx = n_z * n_x * n_y
    rows, width = grad.shape
    rank = inner_ref.shape[0]
    docs = len_ref.shape[1]
    part = width // PARTS
    tokens = n_ctx * rows
    dp = lax.axis_index("dp")
    block = lax.axis_index("ctx")
    z, x, y = block // (n_x * n_y), (block // n_y) % n_x, block % n_y
    n_group = n_dp * n_x
    group = dp * n_x + x

    def along(distance):
        return (dp, lax.rem(block + distance + n_ctx, n_ctx))

    def in_group(g):
        return (g // n_x, z * (n_x * n_y) + lax.rem(g, n_x) * n_y + y)

    def in_z(other):
        return (dp, other * (n_x * n_y) + x * n_y + y)

    def in_y(other):
        return (dp, z * (n_x * n_y) + x * n_y + other)

    smalls = []
    for i, (hbm, ref) in enumerate(
        ((len_hbm, len_ref), (inner_hbm, inner_ref), (inc_hbm, inc_ref))
    ):
        smalls.append(pltpu.make_async_copy(hbm, ref, small_sem.at[i]))
        smalls[-1].start()
    loads = []
    for p in range(PARTS):
        columns = pl.ds(p * part, part)
        loads.append(
            pltpu.make_async_copy(grad_hbm.at[:, columns], grad.at[:, columns], load_sem.at[p])
        )
        loads[-1].start()

    barrier = pltpu.get_barrier_semaphore()
    greeted = 0
    for distance in range(1, REACH + 1):
        for sign in (1, -1):
            pl.semaphore_signal(
                barrier, inc=1, device_id=along(sign * distance), device_id_type=MESH
            )
            greeted += 1
    for size, me, where in ((n_group, group, in_group), (n_z, z, in_z), (n_y, y, in_y)):
        for step in range(1, size):
            pl.semaphore_signal(
                barrier, inc=1, device_id=where(lax.rem(me + step, size)), device_id_type=MESH
            )
            greeted += 1

    for copy in smalls:
        copy.wait()
    lengths = len_ref[...].astype(F32)
    down = lax.broadcasted_iota(jnp.int32, (docs, docs), 0)
    across = lax.broadcasted_iota(jnp.int32, (docs, docs), 1)
    own = down == across
    spread = jnp.broadcast_to(lengths, (docs, docs))
    ends = jnp.sum(jnp.where(across <= down, spread, 0.0), axis=1, keepdims=True)
    length = jnp.sum(jnp.where(own, spread, 0.0), axis=1, keepdims=True)
    start = jnp.min(
        jnp.where(length == LONGEST, ends - length, float(tokens)), axis=0, keepdims=True
    )
    shift = start + off_ref[0].astype(F32)

    def ids_of(positions):
        packed = positions.astype(F32) + shift
        packed = jnp.where(packed >= tokens, packed - tokens, packed)
        return jnp.sum(jnp.where(ends <= packed, 1.0, 0.0), axis=0, keepdims=True)

    ids = ids_of(block * rows + lax.broadcasted_iota(jnp.int32, (1, rows), 1))
    lane = lax.broadcasted_iota(jnp.int32, (1, 128), 1)
    places = jnp.zeros((1, 128), jnp.int32)
    offsets = (-rows - 1, -1, 0, rows, 2 * rows, rows - 1)
    for i, offset in enumerate(offsets):
        places = jnp.where(lane == i, offset, places)
    places = places + block * rows
    places = jnp.where(places < 0, places + tokens, places)
    places = jnp.where(places >= tokens, places - tokens, places)
    edge_ids = ids_of(places)
    behind_2, behind_1, first, ahead_1, ahead_2, last = [
        jnp.sum(jnp.where(lane == i, edge_ids, 0.0), axis=1, keepdims=True)
        for i in range(len(offsets))
    ]

    inner = inner_ref[...].astype(F32)
    local = ids - first
    local = jnp.where(local < 0.0, local + docs, local)
    lhs[0:rank, :] = jnp.where(ids == last, inner, 0.0).astype(BF16)

    def select_docs(begin, end):
        for q in range(begin, end):
            lhs[(q + 1) * rank : (q + 2) * rank, :] = jnp.where(
                local == float(q), inner, 0.0
            ).astype(BF16)

    select_docs(0, 1)

    def halo(p):
        columns = pl.ds(p * part, part)
        far = pl.ds((p % (PARTS // 2)) * part, part)
        low = p < PARTS // 2
        moves = [
            (last_out.at[:, columns], last_in.at[:, columns], along(1)),
            (first_out.at[:, columns], first_in.at[:, columns], along(-1)),
            (last_out.at[:, columns], last_far.at[:, far], along(2))
            if low
            else (first_out.at[:, columns], first_far.at[:, far], along(-2)),
        ]
        return [
            pltpu.make_async_remote_copy(
                src_ref=src,
                dst_ref=dst,
                send_sem=halo_send.at[p, i],
                recv_sem=halo_recv.at[p, i],
                device_id=to,
                device_id_type=MESH,
            )
            for i, (src, dst, to) in enumerate(moves)
        ]

    doc_rows = LOCAL_DOCS * rank
    squares_first = jnp.zeros((rank, 128), F32)
    halos = []
    for p in range(PARTS):
        loads[p].wait()
        columns = slice(p * part, (p + 1) * part)
        sums = jnp.dot(lhs[0 : 2 * rank, :], grad[:, columns], preferred_element_type=F32)
        last_out[:, columns] = sums[0:rank].astype(BF16)
        first_out[:, columns] = sums[rank : 2 * rank].astype(BF16)
        if p == 0:
            pl.semaphore_wait(barrier, greeted)
        halos.append(halo(p))
        for copy in halos[-1]:
            copy.start()
        for tile in lane_tiles(sums[rank : 2 * rank]):
            squares_first = squares_first + tile * tile
    select_docs(1, LOCAL_DOCS)
    squares = jnp.zeros((doc_rows - rank, 128), F32)
    for p in range(PARTS):
        columns = slice(p * part, (p + 1) * part)
        sums = jnp.dot(lhs[2 * rank :, :], grad[:, columns], preferred_element_type=F32)
        for tile in lane_tiles(sums):
            squares = squares + tile * tile
    squares = jnp.concatenate([squares_first, squares], axis=0)

    by_row = jnp.sum(squares, axis=1, keepdims=True)
    label = first + lax.shift_right_logical(
        lax.broadcasted_iota(jnp.int32, (doc_rows, 1), 0), rank.bit_length() - 1
    ).astype(F32)
    label = jnp.where(label >= docs, label - docs, label)
    lane_f = lane.astype(F32)
    terms = jnp.sum(jnp.where(label == lane_f, by_row, 0.0), axis=0, keepdims=True)

    def flag(condition):
        return jnp.where(condition, 2.0, 0.0)

    pair_1 = flag(behind_1 == first)
    pair_2 = flag(behind_1 == ahead_1)
    pair_3_ahead = flag(behind_1 == ahead_2)
    pair_3_behind = flag(behind_2 == ahead_1)
    crossed = jnp.zeros((rank, 128), F32)
    for p in range(PARTS):
        columns = slice(p * part, (p + 1) * part)
        far = slice((p % (PARTS // 2)) * part, (p % (PARTS // 2) + 1) * part)
        for copy in halos[p]:
            copy.wait_recv()
        from_behind = last_in[:, columns].astype(F32)
        from_ahead = first_in[:, columns].astype(F32)
        partner = pair_1 * first_out[:, columns].astype(F32) + pair_2 * from_ahead
        if p < PARTS // 2:
            product = from_behind * partner + (pair_3_behind * from_ahead) * last_far[
                :, far
            ].astype(F32)
        else:
            product = from_behind * (partner + pair_3_ahead * first_far[:, far].astype(F32))
        for tile in lane_tiles(product):
            crossed = crossed + tile
    cross = jnp.sum(jnp.sum(crossed, axis=1, keepdims=True), axis=0, keepdims=True)
    terms = terms + jnp.where(lane_f == first, cross, 0.0)

    terms_out[...] = jnp.broadcast_to(terms, (8, 128))
    news = []
    for distance in range(1, REACH + 1):
        for sign in (1, -1):
            slot = len(news)
            news.append(
                pltpu.make_async_remote_copy(
                    src_ref=terms_out,
                    dst_ref=terms_in.at[slot],
                    send_sem=terms_send.at[slot],
                    recv_sem=terms_recv.at[slot],
                    device_id=along(sign * distance),
                    device_id_type=MESH,
                )
            )
            news[-1].start()
    near = terms
    for slot, copy in enumerate(news):
        copy.wait_recv()
        near = near + terms_in[slot, 0:1, :]
    for step in range(1, n_x):
        slot = len(news)
        news.append(
            pltpu.make_async_remote_copy(
                src_ref=terms_out,
                dst_ref=terms_in.at[slot],
                send_sem=terms_send.at[slot],
                recv_sem=terms_recv.at[slot],
                device_id=in_group(dp * n_x + lax.rem(x + step, n_x)),
                device_id_type=MESH,
            )
        )
        news[-1].start()

    norms = jnp.sqrt(jnp.maximum(near[:, 0:docs], 0.0))
    factor = inc_ref[...].astype(F32) * CLIP_NORM / jnp.maximum(norms, CLIP_NORM)
    factor = jnp.sum(jnp.where(own, jnp.broadcast_to(factor, (docs, docs)), 0.0), axis=1, keepdims=True)
    name = lax.broadcasted_iota(jnp.int32, (docs, 1), 0).astype(F32)
    token_factor = jnp.sum(jnp.where(ids == name, factor, 0.0), axis=0, keepdims=True)
    scaled = (token_factor * inner).astype(BF16)

    each = width // (n_dp * n_ctx)
    run = n_y * each
    slab = n_z * run
    sent = []
    for step in range(1, n_dp + 1):
        to_dp = lax.rem(dp + step, n_dp)
        columns = pl.ds(pl.multiple_of(to_dp * (n_x * slab), 128), n_x * slab)
        sums = jnp.dot(scaled, grad[:, columns], preferred_element_type=F32)
        for other in range(n_x):
            for k in range(n_z):
                column = (k * n_x + other) * run
                clipped[step - 1, other, :, k * run : (k + 1) * run] = sums[:, column : column + run]
        for offset in range(1, n_x + 1):
            if step == n_dp and offset == n_x:
                continue
            to_x = lax.rem(x + offset, n_x)
            slot = len(sent)
            send_1[slot, :, :] = clipped[step - 1, to_x].astype(BF16)
            sent.append(
                pltpu.make_async_remote_copy(
                    src_ref=send_1.at[slot],
                    dst_ref=recv_1.at[slot],
                    send_sem=send_sem_1.at[slot],
                    recv_sem=recv_sem_1.at[slot],
                    device_id=in_group(to_dp * n_x + to_x),
                    device_id_type=MESH,
                )
            )
            sent[-1].start()

    def exchange(size, me, where, out, into, out_sem, in_sem):
        copies = []
        for step in range(1, size):
            to = lax.rem(me + step, size)
            copies.append(
                pltpu.make_async_remote_copy(
                    src_ref=out.at[to],
                    dst_ref=into.at[me],
                    send_sem=out_sem.at[step],
                    recv_sem=in_sem.at[me],
                    device_id=where(to),
                    device_id_type=MESH,
                )
            )
            copies[-1].start()
        into[me] = out[me]
        for step in range(1, size):
            source = lax.rem(me + size - step, size)
            pltpu.make_async_remote_copy(
                src_ref=out.at[source],
                dst_ref=into.at[source],
                send_sem=out_sem.at[step],
                recv_sem=in_sem.at[source],
                device_id=where(source),
                device_id_type=MESH,
            ).wait_recv()
        return copies

    all_terms = terms
    for slot in range(2 * REACH, len(news)):
        news[slot].wait_recv()
        all_terms = all_terms + terms_in[slot, 0:1, :]
    total = clipped[n_dp - 1, x, :, 0:slab]
    for slot, copy in enumerate(sent):
        copy.wait_recv()
        total = total + recv_1[slot, :, 0:slab].astype(F32)
    wide = send_2.shape[2]
    for k in range(n_z):
        send_2[k, :, 0:run] = total[0:8, k * run : (k + 1) * run]
        send_2[k, :, run : 2 * run] = total[8:16, k * run : (k + 1) * run]
        send_2[k, :, wide - docs :] = jnp.broadcast_to(all_terms[:, 0:docs], (8, docs))
    sent += exchange(n_z, z, in_z, send_2, recv_2, send_sem_2, recv_sem_2)
    received = recv_2[0]
    for k in range(1, n_z):
        received = received + recv_2[k]
    for k in range(n_y):
        send_3[k, :, 0:each] = received[:, k * each : (k + 1) * each]
        send_3[k, :, each : 2 * each] = received[:, run + k * each : run + (k + 1) * each]
        send_3[k, :, send_3.shape[2] - docs :] = received[:, wide - docs :]
    sent += exchange(n_y, y, in_y, send_3, recv_3, send_sem_3, recv_sem_3)
    received = recv_3[0]
    for k in range(1, n_y):
        received = received + recv_3[k]
    out_ref[0:8, :] = received[:, 0:each]
    out_ref[8:16, :] = received[:, each : 2 * each]
    norm_ref[...] = jnp.sqrt(jnp.maximum(received[0:1, send_3.shape[2] - docs :], 0.0))

    for copies in halos:
        for copy in copies:
            copy.wait_send()
    for copy in news + sent:
        copy.wait_send()


def on_device(geometry, out_grad, adapter_inner, doc_lengths, slab_offset, included):
    n_dp, n_z, n_x, n_y = geometry
    n_group = n_dp * n_x
    rows, width = out_grad.shape
    rank = adapter_inner.shape[1]
    docs = doc_lengths.shape[1]
    each = width // (n_dp * n_z * n_x * n_y)
    depth = (LOCAL_DOCS + 1) * rank
    long = pl.cdiv(n_z * n_y * each, 128) * 128
    short = pl.cdiv(2 * each + docs, 128) * 128
    wide = pl.cdiv(2 * n_y * each + docs, 128) * 128
    in_vmem = pl.BlockSpec(memory_space=pltpu.VMEM)
    in_hbm = pl.BlockSpec(memory_space=pltpu.HBM)
    dma = pltpu.SemaphoreType.DMA
    gradient, norms = pl.pallas_call(
        functools.partial(kernel, geometry),
        out_shape=(
            jax.ShapeDtypeStruct((rank, each), F32),
            jax.ShapeDtypeStruct((1, docs), F32),
        ),
        in_specs=[
            in_hbm,
            in_hbm,
            in_hbm,
            pl.BlockSpec(memory_space=pltpu.SMEM),
            in_hbm,
        ],
        out_specs=(in_vmem, in_vmem),
        scratch_shapes=[
            pltpu.VMEM((rows, width), BF16),
            pltpu.VMEM((rank, rows), BF16),
            pltpu.VMEM((1, docs), jnp.int32),
            pltpu.VMEM((1, docs), jnp.int32),
            pltpu.VMEM((depth, rows), BF16),
            pltpu.VMEM((rank, width), BF16),
            pltpu.VMEM((rank, width), BF16),
            pltpu.VMEM((rank, width), BF16),
            pltpu.VMEM((rank, width), BF16),
            pltpu.VMEM((rank, width // 2), BF16),
            pltpu.VMEM((rank, width // 2), BF16),
            pltpu.VMEM((8, 128), F32),
            pltpu.VMEM((2 * REACH + n_x - 1, 8, 128), F32),
            pltpu.VMEM((n_dp, n_x, rank, long), F32),
            pltpu.VMEM((n_group - 1, rank, long), BF16),
            pltpu.VMEM((n_group - 1, rank, long), BF16),
            pltpu.VMEM((n_z, 8, wide), F32),
            pltpu.VMEM((n_z, 8, wide), F32),
            pltpu.VMEM((n_y, 8, short), F32),
            pltpu.VMEM((n_y, 8, short), F32),
            dma((PARTS,)),
            dma((3,)),
            dma((PARTS, 3)),
            dma((PARTS, 3)),
            dma((2 * REACH + n_x - 1,)),
            dma((2 * REACH + n_x - 1,)),
            dma((n_group - 1,)),
            dma((n_group - 1,)),
            dma((n_z,)),
            dma((n_z,)),
            dma((n_y,)),
            dma((n_y,)),
        ],
        compiler_params=pltpu.CompilerParams(
            collective_id=0, has_side_effects=True, vmem_limit_bytes=60 * 2**20
        ),
    )(out_grad, adapter_inner.T, doc_lengths, slab_offset, included)
    return gradient.T, norms


def solution(mesh):
    n_x, n_y = 2, 8
    geometry = (mesh.shape["dp"], mesh.shape["ctx"] // (n_x * n_y), n_x, n_y)
    placed = (P(("dp", "ctx"), None), P(("dp", "ctx"), None), P("dp", None), P("dp"), P("dp", None))
    return jax.shard_map(
        functools.partial(on_device, geometry),
        mesh=mesh,
        in_specs=placed,
        out_specs=(P(("dp", "ctx"), None), P("dp", None)),
        check_vma=False,
    )
```

```python
import functools

import jax
import jax.numpy as jnp
from jax import lax
from jax.experimental import pallas as pl
from jax.experimental.pallas import tpu as pltpu
from jax.sharding import PartitionSpec as P

CLIP_NORM = 128.0
LONGEST = 1536.0
LOCAL_DOCS = 23
REACH = 3
PARTS = 4
MESH = pl.DeviceIdType.MESH
F32 = jnp.float32
BF16 = jnp.bfloat16


def lane_tiles(array):
    return [array[:, k : k + 128] for k in range(0, array.shape[1], 128)]


def kernel(
    geometry, grad_hbm, inner_hbm, len_hbm, off_ref, inc_hbm,
    out_ref, norm_ref,
    grad, inner_ref, len_ref, inc_ref, lhs, last_out, first_out, last_in, first_in, last_far, first_far,
    terms_out, terms_in, clipped, send_1, recv_1, send_2, recv_2, send_3, recv_3,
    load_sem, small_sem, halo_send, halo_recv, terms_send, terms_recv,
    send_sem_1, recv_sem_1, send_sem_2, recv_sem_2, send_sem_3, recv_sem_3,
):
    n_dp, n_z, n_x, n_y = geometry
    n_ctx = n_z * n_x * n_y
    rows, width = grad.shape
    rank = inner_ref.shape[0]
    docs = len_ref.shape[1]
    part = width // PARTS
    tokens = n_ctx * rows
    dp = lax.axis_index("dp")
    block = lax.axis_index("ctx")
    z, x, y = block // (n_x * n_y), (block // n_y) % n_x, block % n_y
    n_group = n_dp * n_x
    group = dp * n_x + x

    def along(distance):
        return (dp, lax.rem(block + distance + n_ctx, n_ctx))

    def in_group(g):
        return (g // n_x, z * (n_x * n_y) + lax.rem(g, n_x) * n_y + y)

    def in_z(other):
        return (dp, other * (n_x * n_y) + x * n_y + y)

    def in_y(other):
        return (dp, z * (n_x * n_y) + x * n_y + other)

    smalls = []
    for i, (hbm, ref) in enumerate(
        ((len_hbm, len_ref), (inner_hbm, inner_ref), (inc_hbm, inc_ref))
    ):
        smalls.append(pltpu.make_async_copy(hbm, ref, small_sem.at[i]))
        smalls[-1].start()
    loads = []
    for p in range(PARTS):
        columns = pl.ds(p * part, part)
        loads.append(
            pltpu.make_async_copy(grad_hbm.at[:, columns], grad.at[:, columns], load_sem.at[p])
        )
        loads[-1].start()

    barrier = pltpu.get_barrier_semaphore()
    greeted = 0
    for distance in range(1, REACH + 1):
        for sign in (1, -1):
            pl.semaphore_signal(
                barrier, inc=1, device_id=along(sign * distance), device_id_type=MESH
            )
            greeted += 1
    for size, me, where in ((n_group, group, in_group), (n_z, z, in_z), (n_y, y, in_y)):
        for step in range(1, size):
            pl.semaphore_signal(
                barrier, inc=1, device_id=where(lax.rem(me + step, size)), device_id_type=MESH
            )
            greeted += 1

    for copy in smalls:
        copy.wait()
    lengths = len_ref[...].astype(F32)
    down = lax.broadcasted_iota(jnp.int32, (docs, docs), 0)
    across = lax.broadcasted_iota(jnp.int32, (docs, docs), 1)
    own = down == across
    spread = jnp.broadcast_to(lengths, (docs, docs))
    ends = jnp.sum(jnp.where(across <= down, spread, 0.0), axis=1, keepdims=True)
    length = jnp.sum(jnp.where(own, spread, 0.0), axis=1, keepdims=True)
    start = jnp.min(
        jnp.where(length == LONGEST, ends - length, float(tokens)), axis=0, keepdims=True
    )
    shift = start + off_ref[0].astype(F32)

    def ids_of(positions):
        packed = positions.astype(F32) + shift
        packed = jnp.where(packed >= tokens, packed - tokens, packed)
        return jnp.sum(jnp.where(ends <= packed, 1.0, 0.0), axis=0, keepdims=True)

    ids = ids_of(block * rows + lax.broadcasted_iota(jnp.int32, (1, rows), 1))
    lane = lax.broadcasted_iota(jnp.int32, (1, 128), 1)
    places = jnp.zeros((1, 128), jnp.int32)
    offsets = (-rows - 1, -1, 0, rows, 2 * rows, rows - 1)
    for i, offset in enumerate(offsets):
        places = jnp.where(lane == i, offset, places)
    places = places + block * rows
    places = jnp.where(places < 0, places + tokens, places)
    places = jnp.where(places >= tokens, places - tokens, places)
    edge_ids = ids_of(places)
    behind_2, behind_1, first, ahead_1, ahead_2, last = [
        jnp.sum(jnp.where(lane == i, edge_ids, 0.0), axis=1, keepdims=True)
        for i in range(len(offsets))
    ]

    inner = inner_ref[...].astype(F32)
    local = ids - first
    local = jnp.where(local < 0.0, local + docs, local)
    lhs[0:rank, :] = jnp.where(ids == last, inner, 0.0).astype(BF16)

    def select_docs(begin, end):
        for q in range(begin, end):
            lhs[(q + 1) * rank : (q + 2) * rank, :] = jnp.where(
                local == float(q), inner, 0.0
            ).astype(BF16)

    select_docs(0, 1)

    low = range(PARTS // 2)
    high = range(PARTS // 2, PARTS)

    def move(kind, p):
        columns = pl.ds(p * part, part)
        far = pl.ds((p % (PARTS // 2)) * part, part)
        src, dst, to = {
            "last": (last_out.at[:, columns], last_in.at[:, columns], along(1)),
            "first": (first_out.at[:, columns], first_in.at[:, columns], along(-1)),
            "on": (last_in.at[:, columns], last_far.at[:, far], along(1))
            if p in low
            else (first_in.at[:, columns], first_far.at[:, far], along(-1)),
        }[kind]
        slot = ("last", "first", "on").index(kind)
        return pltpu.make_async_remote_copy(
            src_ref=src,
            dst_ref=dst,
            send_sem=halo_send.at[p, slot],
            recv_sem=halo_recv.at[p, slot],
            device_id=to,
            device_id_type=MESH,
        )

    doc_rows = LOCAL_DOCS * rank
    squares_first = jnp.zeros((rank, 128), F32)
    halos = {(kind, p): move(kind, p) for kind in ("last", "first", "on") for p in range(PARTS)}
    begun = 0
    for p in [q for pair in zip(low, high) for q in pair]:
        loads[p].wait()
        columns = slice(p * part, (p + 1) * part)
        sums = jnp.dot(lhs[0 : 2 * rank, :], grad[:, columns], preferred_element_type=F32)
        last_out[:, columns] = sums[0:rank].astype(BF16)
        first_out[:, columns] = sums[rank : 2 * rank].astype(BF16)
        if begun == 0:
            pl.semaphore_wait(barrier, greeted)
        begun += 1
        halos["last" if p in low else "first", p].start()
        for tile in lane_tiles(sums[rank : 2 * rank]):
            squares_first = squares_first + tile * tile
    for p, q in zip(low, high):
        halos["first", p].start()
        halos["last", q].start()
    select_docs(1, LOCAL_DOCS)
    squares = jnp.zeros((doc_rows - rank, 128), F32)
    for p in range(PARTS):
        if p >= PARTS // 2:
            halos["last", p - PARTS // 2].wait_recv()
            halos["on", p - PARTS // 2].start()
            halos["first", p].wait_recv()
            halos["on", p].start()
        columns = slice(p * part, (p + 1) * part)
        sums = jnp.dot(lhs[2 * rank :, :], grad[:, columns], preferred_element_type=F32)
        for tile in lane_tiles(sums):
            squares = squares + tile * tile
    squares = jnp.concatenate([squares_first, squares], axis=0)

    by_row = jnp.sum(squares, axis=1, keepdims=True)
    label = first + lax.shift_right_logical(
        lax.broadcasted_iota(jnp.int32, (doc_rows, 1), 0), rank.bit_length() - 1
    ).astype(F32)
    label = jnp.where(label >= docs, label - docs, label)
    lane_f = lane.astype(F32)
    terms = jnp.sum(jnp.where(label == lane_f, by_row, 0.0), axis=0, keepdims=True)

    def flag(condition):
        return jnp.where(condition, 2.0, 0.0)

    pair_1 = flag(behind_1 == first)
    pair_2 = flag(behind_1 == ahead_1)
    pair_3_ahead = flag(behind_1 == ahead_2)
    pair_3_behind = flag(behind_2 == ahead_1)
    crossed = jnp.zeros((rank, 128), F32)
    for p in range(PARTS):
        columns = slice(p * part, (p + 1) * part)
        far = slice((p % (PARTS // 2)) * part, (p % (PARTS // 2) + 1) * part)
        halos["first" if p in low else "last", p].wait_recv()
        halos["on", p].wait_recv()
        from_behind = last_in[:, columns].astype(F32)
        from_ahead = first_in[:, columns].astype(F32)
        partner = pair_1 * first_out[:, columns].astype(F32) + pair_2 * from_ahead
        if p in low:
            product = from_behind * partner + (pair_3_behind * from_ahead) * last_far[
                :, far
            ].astype(F32)
        else:
            product = from_behind * (partner + pair_3_ahead * first_far[:, far].astype(F32))
        for tile in lane_tiles(product):
            crossed = crossed + tile
    cross = jnp.sum(jnp.sum(crossed, axis=1, keepdims=True), axis=0, keepdims=True)
    terms = terms + jnp.where(lane_f == first, cross, 0.0)

    terms_out[...] = jnp.broadcast_to(terms, (8, 128))
    news = []
    for distance in range(1, REACH + 1):
        for sign in (1, -1):
            slot = len(news)
            news.append(
                pltpu.make_async_remote_copy(
                    src_ref=terms_out,
                    dst_ref=terms_in.at[slot],
                    send_sem=terms_send.at[slot],
                    recv_sem=terms_recv.at[slot],
                    device_id=along(sign * distance),
                    device_id_type=MESH,
                )
            )
            news[-1].start()
    near = terms
    for slot, copy in enumerate(news):
        copy.wait_recv()
        near = near + terms_in[slot, 0:1, :]
    for step in range(1, n_x):
        slot = len(news)
        news.append(
            pltpu.make_async_remote_copy(
                src_ref=terms_out,
                dst_ref=terms_in.at[slot],
                send_sem=terms_send.at[slot],
                recv_sem=terms_recv.at[slot],
                device_id=in_group(dp * n_x + lax.rem(x + step, n_x)),
                device_id_type=MESH,
            )
        )
        news[-1].start()

    norms = jnp.sqrt(jnp.maximum(near[:, 0:docs], 0.0))
    factor = inc_ref[...].astype(F32) * CLIP_NORM / jnp.maximum(norms, CLIP_NORM)
    factor = jnp.sum(jnp.where(own, jnp.broadcast_to(factor, (docs, docs)), 0.0), axis=1, keepdims=True)
    name = lax.broadcasted_iota(jnp.int32, (docs, 1), 0).astype(F32)
    token_factor = jnp.sum(jnp.where(ids == name, factor, 0.0), axis=0, keepdims=True)
    scaled = (token_factor * inner).astype(BF16)

    each = width // (n_dp * n_ctx)
    run = n_y * each
    slab = n_z * run
    sent = []
    for step in range(1, n_dp + 1):
        to_dp = lax.rem(dp + step, n_dp)
        columns = pl.ds(pl.multiple_of(to_dp * (n_x * slab), 128), n_x * slab)
        sums = jnp.dot(scaled, grad[:, columns], preferred_element_type=F32)
        for other in range(n_x):
            for k in range(n_z):
                column = (k * n_x + other) * run
                clipped[step - 1, other, :, k * run : (k + 1) * run] = sums[:, column : column + run]
        for offset in range(1, n_x + 1):
            if step == n_dp and offset == n_x:
                continue
            to_x = lax.rem(x + offset, n_x)
            slot = len(sent)
            send_1[slot, :, :] = clipped[step - 1, to_x].astype(BF16)
            sent.append(
                pltpu.make_async_remote_copy(
                    src_ref=send_1.at[slot],
                    dst_ref=recv_1.at[slot],
                    send_sem=send_sem_1.at[slot],
                    recv_sem=recv_sem_1.at[slot],
                    device_id=in_group(to_dp * n_x + to_x),
                    device_id_type=MESH,
                )
            )
            sent[-1].start()

    def exchange(size, me, where, out, into, out_sem, in_sem):
        copies = []
        for step in range(1, size):
            to = lax.rem(me + step, size)
            copies.append(
                pltpu.make_async_remote_copy(
                    src_ref=out.at[to],
                    dst_ref=into.at[me],
                    send_sem=out_sem.at[step],
                    recv_sem=in_sem.at[me],
                    device_id=where(to),
                    device_id_type=MESH,
                )
            )
            copies[-1].start()
        into[me] = out[me]
        for step in range(1, size):
            source = lax.rem(me + size - step, size)
            pltpu.make_async_remote_copy(
                src_ref=out.at[source],
                dst_ref=into.at[source],
                send_sem=out_sem.at[step],
                recv_sem=in_sem.at[source],
                device_id=where(source),
                device_id_type=MESH,
            ).wait_recv()
        return copies

    all_terms = terms
    for slot in range(2 * REACH, len(news)):
        news[slot].wait_recv()
        all_terms = all_terms + terms_in[slot, 0:1, :]
    total = clipped[n_dp - 1, x, :, 0:slab]
    for slot, copy in enumerate(sent):
        copy.wait_recv()
        total = total + recv_1[slot, :, 0:slab].astype(F32)
    wide = send_2.shape[2]
    for k in range(n_z):
        send_2[k, :, 0:run] = total[0:8, k * run : (k + 1) * run]
        send_2[k, :, run : 2 * run] = total[8:16, k * run : (k + 1) * run]
        send_2[k, :, wide - docs :] = jnp.broadcast_to(all_terms[:, 0:docs], (8, docs))
    sent += exchange(n_z, z, in_z, send_2, recv_2, send_sem_2, recv_sem_2)
    received = recv_2[0]
    for k in range(1, n_z):
        received = received + recv_2[k]
    for k in range(n_y):
        send_3[k, :, 0:each] = received[:, k * each : (k + 1) * each]
        send_3[k, :, each : 2 * each] = received[:, run + k * each : run + (k + 1) * each]
        send_3[k, :, send_3.shape[2] - docs :] = received[:, wide - docs :]
    sent += exchange(n_y, y, in_y, send_3, recv_3, send_sem_3, recv_sem_3)
    received = recv_3[0]
    for k in range(1, n_y):
        received = received + recv_3[k]
    out_ref[0:8, :] = received[:, 0:each]
    out_ref[8:16, :] = received[:, each : 2 * each]
    norm_ref[...] = jnp.sqrt(jnp.maximum(received[0:1, send_3.shape[2] - docs :], 0.0))

    for copy in [*halos.values(), *news, *sent]:
        copy.wait_send()


def on_device(geometry, out_grad, adapter_inner, doc_lengths, slab_offset, included):
    n_dp, n_z, n_x, n_y = geometry
    n_group = n_dp * n_x
    rows, width = out_grad.shape
    rank = adapter_inner.shape[1]
    docs = doc_lengths.shape[1]
    each = width // (n_dp * n_z * n_x * n_y)
    depth = (LOCAL_DOCS + 1) * rank
    long = pl.cdiv(n_z * n_y * each, 128) * 128
    short = pl.cdiv(2 * each + docs, 128) * 128
    wide = pl.cdiv(2 * n_y * each + docs, 128) * 128
    in_vmem = pl.BlockSpec(memory_space=pltpu.VMEM)
    in_hbm = pl.BlockSpec(memory_space=pltpu.HBM)
    dma = pltpu.SemaphoreType.DMA
    gradient, norms = pl.pallas_call(
        functools.partial(kernel, geometry),
        out_shape=(
            jax.ShapeDtypeStruct((rank, each), F32),
            jax.ShapeDtypeStruct((1, docs), F32),
        ),
        in_specs=[
            in_hbm,
            in_hbm,
            in_hbm,
            pl.BlockSpec(memory_space=pltpu.SMEM),
            in_hbm,
        ],
        out_specs=(in_vmem, in_vmem),
        scratch_shapes=[
            pltpu.VMEM((rows, width), BF16),
            pltpu.VMEM((rank, rows), BF16),
            pltpu.VMEM((1, docs), jnp.int32),
            pltpu.VMEM((1, docs), jnp.int32),
            pltpu.VMEM((depth, rows), BF16),
            pltpu.VMEM((rank, width), BF16),
            pltpu.VMEM((rank, width), BF16),
            pltpu.VMEM((rank, width), BF16),
            pltpu.VMEM((rank, width), BF16),
            pltpu.VMEM((rank, width // 2), BF16),
            pltpu.VMEM((rank, width // 2), BF16),
            pltpu.VMEM((8, 128), F32),
            pltpu.VMEM((2 * REACH + n_x - 1, 8, 128), F32),
            pltpu.VMEM((n_dp, n_x, rank, long), F32),
            pltpu.VMEM((n_group - 1, rank, long), BF16),
            pltpu.VMEM((n_group - 1, rank, long), BF16),
            pltpu.VMEM((n_z, 8, wide), F32),
            pltpu.VMEM((n_z, 8, wide), F32),
            pltpu.VMEM((n_y, 8, short), F32),
            pltpu.VMEM((n_y, 8, short), F32),
            dma((PARTS,)),
            dma((3,)),
            dma((PARTS, 3)),
            dma((PARTS, 3)),
            dma((2 * REACH + n_x - 1,)),
            dma((2 * REACH + n_x - 1,)),
            dma((n_group - 1,)),
            dma((n_group - 1,)),
            dma((n_z,)),
            dma((n_z,)),
            dma((n_y,)),
            dma((n_y,)),
        ],
        compiler_params=pltpu.CompilerParams(
            collective_id=0, has_side_effects=True, vmem_limit_bytes=60 * 2**20
        ),
    )(out_grad, adapter_inner.T, doc_lengths, slab_offset, included)
    return gradient.T, norms


def solution(mesh):
    n_x, n_y = 2, 8
    geometry = (mesh.shape["dp"], mesh.shape["ctx"] // (n_x * n_y), n_x, n_y)
    placed = (P(("dp", "ctx"), None), P(("dp", "ctx"), None), P("dp", None), P("dp"), P("dp", None))
    return jax.shard_map(
        functools.partial(on_device, geometry),
        mesh=mesh,
        in_specs=placed,
        out_specs=(P(("dp", "ctx"), None), P("dp", None)),
        check_vma=False,
    )
```

```python
import functools

import jax
import jax.numpy as jnp
from jax import lax
from jax.experimental import pallas as pl
from jax.experimental.pallas import tpu as pltpu
from jax.sharding import PartitionSpec as P

CLIP_NORM = 128.0
LONGEST = 1536.0
LOCAL_DOCS = 23
REACH = 3
PARTS = 4
STRIP = 512
MESH = pl.DeviceIdType.MESH
F32 = jnp.float32
BF16 = jnp.bfloat16


def lane_tiles(array):
    return [array[:, k : k + 128] for k in range(0, array.shape[1], 128)]


def kernel(
    geometry, grad_hbm, inner_hbm, len_hbm, off_ref, inc_hbm,
    out_ref, norm_ref,
    grad, inner_ref, len_ref, inc_ref, lhs, last_out, first_out, last_in, first_in, last_far, first_far,
    terms_out, terms_in, clipped, send_1, recv_1, send_2, recv_2, send_3, recv_3,
    load_sem, small_sem, halo_send, halo_recv, terms_send, terms_recv,
    send_sem_1, recv_sem_1, send_sem_2, recv_sem_2, send_sem_3, recv_sem_3,
):
    n_dp, n_z, n_x, n_y = geometry
    n_ctx = n_z * n_x * n_y
    rows, width = grad.shape
    rank = inner_ref.shape[0]
    docs = len_ref.shape[1]
    part = width // PARTS
    tokens = n_ctx * rows
    dp = lax.axis_index("dp")
    block = lax.axis_index("ctx")
    z, x, y = block // (n_x * n_y), (block // n_y) % n_x, block % n_y
    n_group = n_dp * n_x
    group = dp * n_x + x

    def along(distance):
        return (dp, lax.rem(block + distance + n_ctx, n_ctx))

    def in_group(g):
        return (g // n_x, z * (n_x * n_y) + lax.rem(g, n_x) * n_y + y)

    def in_z(other):
        return (dp, other * (n_x * n_y) + x * n_y + y)

    def in_y(other):
        return (dp, z * (n_x * n_y) + x * n_y + other)

    smalls = []
    for i, (hbm, ref) in enumerate(
        ((len_hbm, len_ref), (inner_hbm, inner_ref), (inc_hbm, inc_ref))
    ):
        smalls.append(pltpu.make_async_copy(hbm, ref, small_sem.at[i]))
        smalls[-1].start()
    loads = []
    for p in range(PARTS):
        columns = pl.ds(p * part, part)
        loads.append(
            pltpu.make_async_copy(grad_hbm.at[:, columns], grad.at[:, columns], load_sem.at[p])
        )
        loads[-1].start()

    barrier = pltpu.get_barrier_semaphore()
    greeted = 0
    for distance in range(1, REACH + 1):
        for sign in (1, -1):
            pl.semaphore_signal(
                barrier, inc=1, device_id=along(sign * distance), device_id_type=MESH
            )
            greeted += 1
    for size, me, where in ((n_group, group, in_group), (n_z, z, in_z), (n_y, y, in_y)):
        for step in range(1, size):
            pl.semaphore_signal(
                barrier, inc=1, device_id=where(lax.rem(me + step, size)), device_id_type=MESH
            )
            greeted += 1

    for copy in smalls:
        copy.wait()
    lengths = len_ref[...].astype(F32)
    down = lax.broadcasted_iota(jnp.int32, (docs, docs), 0)
    across = lax.broadcasted_iota(jnp.int32, (docs, docs), 1)
    own = down == across
    spread = jnp.broadcast_to(lengths, (docs, docs))
    ends = jnp.sum(jnp.where(across <= down, spread, 0.0), axis=1, keepdims=True)
    length = jnp.sum(jnp.where(own, spread, 0.0), axis=1, keepdims=True)
    start = jnp.min(
        jnp.where(length == LONGEST, ends - length, float(tokens)), axis=0, keepdims=True
    )
    shift = start + off_ref[0].astype(F32)

    def ids_of(positions):
        packed = positions.astype(F32) + shift
        packed = jnp.where(packed >= tokens, packed - tokens, packed)
        return jnp.sum(jnp.where(ends <= packed, 1.0, 0.0), axis=0, keepdims=True)

    ids = ids_of(block * rows + lax.broadcasted_iota(jnp.int32, (1, rows), 1))
    lane = lax.broadcasted_iota(jnp.int32, (1, 128), 1)
    places = jnp.zeros((1, 128), jnp.int32)
    offsets = (-rows - 1, -1, 0, rows, 2 * rows, rows - 1)
    for i, offset in enumerate(offsets):
        places = jnp.where(lane == i, offset, places)
    places = places + block * rows
    places = jnp.where(places < 0, places + tokens, places)
    places = jnp.where(places >= tokens, places - tokens, places)
    edge_ids = ids_of(places)
    behind_2, behind_1, first, ahead_1, ahead_2, last = [
        jnp.sum(jnp.where(lane == i, edge_ids, 0.0), axis=1, keepdims=True)
        for i in range(len(offsets))
    ]

    inner = inner_ref[...].astype(F32)
    local = ids - first
    local = jnp.where(local < 0.0, local + docs, local)
    lhs[0:rank, :] = jnp.where(ids == last, inner, 0.0).astype(BF16)

    def select_docs(begin, end):
        for q in range(begin, end):
            lhs[(q + 1) * rank : (q + 2) * rank, :] = jnp.where(
                local == float(q), inner, 0.0
            ).astype(BF16)

    select_docs(0, 1)

    def halo(p):
        columns = pl.ds(p * part, part)
        far = pl.ds((p % (PARTS // 2)) * part, part)
        low = p < PARTS // 2
        moves = [
            (last_out.at[:, columns], last_in.at[:, columns], along(1)),
            (first_out.at[:, columns], first_in.at[:, columns], along(-1)),
            (last_out.at[:, columns], last_far.at[:, far], along(2))
            if low
            else (first_out.at[:, columns], first_far.at[:, far], along(-2)),
        ]
        return [
            pltpu.make_async_remote_copy(
                src_ref=src,
                dst_ref=dst,
                send_sem=halo_send.at[p, i],
                recv_sem=halo_recv.at[p, i],
                device_id=to,
                device_id_type=MESH,
            )
            for i, (src, dst, to) in enumerate(moves)
        ]

    doc_rows = LOCAL_DOCS * rank
    squares_first = jnp.zeros((rank, 128), F32)
    halos = []
    for p in range(PARTS):
        loads[p].wait()
        columns = slice(p * part, (p + 1) * part)
        sums = jnp.dot(lhs[0 : 2 * rank, :], grad[:, columns], preferred_element_type=F32)
        last_out[:, columns] = sums[0:rank].astype(BF16)
        first_out[:, columns] = sums[rank : 2 * rank].astype(BF16)
        if p == 0:
            pl.semaphore_wait(barrier, greeted)
        halos.append(halo(p))
        for copy in halos[-1]:
            copy.start()
        for tile in lane_tiles(sums[rank : 2 * rank]):
            squares_first = squares_first + tile * tile
    select_docs(1, LOCAL_DOCS)

    def add_squares(i, squares):
        columns = pl.ds(pl.multiple_of(i * STRIP, 128), STRIP)
        sums = jnp.dot(lhs[2 * rank :, :], grad[:, columns], preferred_element_type=F32)
        for tile in lane_tiles(sums):
            squares = squares + tile * tile
        return squares

    squares = jnp.zeros((doc_rows - rank, 128), F32)
    squares = lax.fori_loop(0, width // STRIP, add_squares, squares)
    squares = jnp.concatenate([squares_first, squares], axis=0)

    by_row = jnp.sum(squares, axis=1, keepdims=True)
    label = first + lax.shift_right_logical(
        lax.broadcasted_iota(jnp.int32, (doc_rows, 1), 0), rank.bit_length() - 1
    ).astype(F32)
    label = jnp.where(label >= docs, label - docs, label)
    lane_f = lane.astype(F32)
    terms = jnp.sum(jnp.where(label == lane_f, by_row, 0.0), axis=0, keepdims=True)

    def flag(condition):
        return jnp.where(condition, 2.0, 0.0)

    pair_1 = flag(behind_1 == first)
    pair_2 = flag(behind_1 == ahead_1)
    pair_3_ahead = flag(behind_1 == ahead_2)
    pair_3_behind = flag(behind_2 == ahead_1)
    crossed = jnp.zeros((rank, 128), F32)
    for p in range(PARTS):
        columns = slice(p * part, (p + 1) * part)
        far = slice((p % (PARTS // 2)) * part, (p % (PARTS // 2) + 1) * part)
        for copy in halos[p]:
            copy.wait_recv()
        from_behind = last_in[:, columns].astype(F32)
        from_ahead = first_in[:, columns].astype(F32)
        partner = pair_1 * first_out[:, columns].astype(F32) + pair_2 * from_ahead
        if p < PARTS // 2:
            product = from_behind * partner + (pair_3_behind * from_ahead) * last_far[
                :, far
            ].astype(F32)
        else:
            product = from_behind * (partner + pair_3_ahead * first_far[:, far].astype(F32))
        for tile in lane_tiles(product):
            crossed = crossed + tile
    cross = jnp.sum(jnp.sum(crossed, axis=1, keepdims=True), axis=0, keepdims=True)
    terms = terms + jnp.where(lane_f == first, cross, 0.0)

    terms_out[...] = jnp.broadcast_to(terms, (8, 128))
    news = []
    for distance in range(1, REACH + 1):
        for sign in (1, -1):
            slot = len(news)
            news.append(
                pltpu.make_async_remote_copy(
                    src_ref=terms_out,
                    dst_ref=terms_in.at[slot],
                    send_sem=terms_send.at[slot],
                    recv_sem=terms_recv.at[slot],
                    device_id=along(sign * distance),
                    device_id_type=MESH,
                )
            )
            news[-1].start()
    near = terms
    for slot, copy in enumerate(news):
        copy.wait_recv()
        near = near + terms_in[slot, 0:1, :]
    for step in range(1, n_x):
        slot = len(news)
        news.append(
            pltpu.make_async_remote_copy(
                src_ref=terms_out,
                dst_ref=terms_in.at[slot],
                send_sem=terms_send.at[slot],
                recv_sem=terms_recv.at[slot],
                device_id=in_group(dp * n_x + lax.rem(x + step, n_x)),
                device_id_type=MESH,
            )
        )
        news[-1].start()

    norms = jnp.sqrt(jnp.maximum(near[:, 0:docs], 0.0))
    factor = inc_ref[...].astype(F32) * CLIP_NORM / jnp.maximum(norms, CLIP_NORM)
    factor = jnp.sum(jnp.where(own, jnp.broadcast_to(factor, (docs, docs)), 0.0), axis=1, keepdims=True)
    name = lax.broadcasted_iota(jnp.int32, (docs, 1), 0).astype(F32)
    token_factor = jnp.sum(jnp.where(ids == name, factor, 0.0), axis=0, keepdims=True)
    scaled = (token_factor * inner).astype(BF16)

    each = width // (n_dp * n_ctx)
    run = n_y * each
    slab = n_z * run

    def share(step, offset):
        slot = (step - 1) * n_x + offset - 1
        to = lax.rem(dp + step, n_dp) * n_x + lax.rem(x + offset, n_x)
        return pltpu.make_async_remote_copy(
            src_ref=send_1.at[slot],
            dst_ref=recv_1.at[slot],
            send_sem=send_sem_1.at[slot],
            recv_sem=recv_sem_1.at[slot],
            device_id=in_group(to),
            device_id_type=MESH,
        )

    def multiply(step, offsets):
        to_dp = lax.rem(dp + step, n_dp)
        columns = pl.ds(pl.multiple_of(to_dp * (n_x * slab), 128), n_x * slab)
        sums = jnp.dot(scaled, grad[:, columns], preferred_element_type=F32)
        for other in range(n_x):
            for k in range(n_z):
                column = (k * n_x + other) * run
                clipped[other, :, k * run : (k + 1) * run] = sums[:, column : column + run]
        for offset in offsets:
            slot = (step - 1) * n_x + offset - 1
            send_1[slot] = clipped[lax.rem(x + offset, n_x)].astype(BF16)
            share(step, offset).start()

    @pl.loop(1, n_dp)
    def _(step):
        multiply(step, range(1, n_x + 1))

    multiply(n_dp, range(1, n_x))
    sent = [
        share(step, offset)
        for step in range(1, n_dp + 1)
        for offset in range(1, n_x + 1)
        if (step, offset) != (n_dp, n_x)
    ]

    def exchange(size, me, where, out, into, out_sem, in_sem):
        copies = []
        for step in range(1, size):
            to = lax.rem(me + step, size)
            copies.append(
                pltpu.make_async_remote_copy(
                    src_ref=out.at[to],
                    dst_ref=into.at[me],
                    send_sem=out_sem.at[step],
                    recv_sem=in_sem.at[me],
                    device_id=where(to),
                    device_id_type=MESH,
                )
            )
            copies[-1].start()
        into[me] = out[me]
        for step in range(1, size):
            source = lax.rem(me + size - step, size)
            pltpu.make_async_remote_copy(
                src_ref=out.at[source],
                dst_ref=into.at[source],
                send_sem=out_sem.at[step],
                recv_sem=in_sem.at[source],
                device_id=where(source),
                device_id_type=MESH,
            ).wait_recv()
        return copies

    all_terms = terms
    for slot in range(2 * REACH, len(news)):
        news[slot].wait_recv()
        all_terms = all_terms + terms_in[slot, 0:1, :]
    total = clipped[x, :, 0:slab]
    for slot, copy in enumerate(sent):
        copy.wait_recv()
        total = total + recv_1[slot, :, 0:slab].astype(F32)
    wide = send_2.shape[2]
    for k in range(n_z):
        send_2[k, :, 0:run] = total[0:8, k * run : (k + 1) * run]
        send_2[k, :, run : 2 * run] = total[8:16, k * run : (k + 1) * run]
        send_2[k, :, wide - docs :] = jnp.broadcast_to(all_terms[:, 0:docs], (8, docs))
    sent += exchange(n_z, z, in_z, send_2, recv_2, send_sem_2, recv_sem_2)
    received = recv_2[0]
    for k in range(1, n_z):
        received = received + recv_2[k]
    for k in range(n_y):
        send_3[k, :, 0:each] = received[:, k * each : (k + 1) * each]
        send_3[k, :, each : 2 * each] = received[:, run + k * each : run + (k + 1) * each]
        send_3[k, :, send_3.shape[2] - docs :] = received[:, wide - docs :]
    sent += exchange(n_y, y, in_y, send_3, recv_3, send_sem_3, recv_sem_3)
    received = recv_3[0]
    for k in range(1, n_y):
        received = received + recv_3[k]
    out_ref[0:8, :] = received[:, 0:each]
    out_ref[8:16, :] = received[:, each : 2 * each]
    norm_ref[...] = jnp.sqrt(jnp.maximum(received[0:1, send_3.shape[2] - docs :], 0.0))

    for copies in halos:
        for copy in copies:
            copy.wait_send()
    for copy in news + sent:
        copy.wait_send()


def on_device(geometry, out_grad, adapter_inner, doc_lengths, slab_offset, included):
    n_dp, n_z, n_x, n_y = geometry
    n_group = n_dp * n_x
    rows, width = out_grad.shape
    rank = adapter_inner.shape[1]
    docs = doc_lengths.shape[1]
    each = width // (n_dp * n_z * n_x * n_y)
    depth = (LOCAL_DOCS + 1) * rank
    long = pl.cdiv(n_z * n_y * each, 128) * 128
    short = pl.cdiv(2 * each + docs, 128) * 128
    wide = pl.cdiv(2 * n_y * each + docs, 128) * 128
    in_vmem = pl.BlockSpec(memory_space=pltpu.VMEM)
    in_hbm = pl.BlockSpec(memory_space=pltpu.HBM)
    dma = pltpu.SemaphoreType.DMA
    gradient, norms = pl.pallas_call(
        functools.partial(kernel, geometry),
        out_shape=(
            jax.ShapeDtypeStruct((rank, each), F32),
            jax.ShapeDtypeStruct((1, docs), F32),
        ),
        in_specs=[
            in_hbm,
            in_hbm,
            in_hbm,
            pl.BlockSpec(memory_space=pltpu.SMEM),
            in_hbm,
        ],
        out_specs=(in_vmem, in_vmem),
        scratch_shapes=[
            pltpu.VMEM((rows, width), BF16),
            pltpu.VMEM((rank, rows), BF16),
            pltpu.VMEM((1, docs), jnp.int32),
            pltpu.VMEM((1, docs), jnp.int32),
            pltpu.VMEM((depth, rows), BF16),
            pltpu.VMEM((rank, width), BF16),
            pltpu.VMEM((rank, width), BF16),
            pltpu.VMEM((rank, width), BF16),
            pltpu.VMEM((rank, width), BF16),
            pltpu.VMEM((rank, width // 2), BF16),
            pltpu.VMEM((rank, width // 2), BF16),
            pltpu.VMEM((8, 128), F32),
            pltpu.VMEM((2 * REACH + n_x - 1, 8, 128), F32),
            pltpu.VMEM((n_x, rank, long), F32),
            pltpu.VMEM((n_group - 1, rank, long), BF16),
            pltpu.VMEM((n_group - 1, rank, long), BF16),
            pltpu.VMEM((n_z, 8, wide), F32),
            pltpu.VMEM((n_z, 8, wide), F32),
            pltpu.VMEM((n_y, 8, short), F32),
            pltpu.VMEM((n_y, 8, short), F32),
            dma((PARTS,)),
            dma((3,)),
            dma((PARTS, 3)),
            dma((PARTS, 3)),
            dma((2 * REACH + n_x - 1,)),
            dma((2 * REACH + n_x - 1,)),
            dma((n_group - 1,)),
            dma((n_group - 1,)),
            dma((n_z,)),
            dma((n_z,)),
            dma((n_y,)),
            dma((n_y,)),
        ],
        compiler_params=pltpu.CompilerParams(
            collective_id=0, has_side_effects=True, vmem_limit_bytes=60 * 2**20
        ),
    )(out_grad, adapter_inner.T, doc_lengths, slab_offset, included)
    return gradient.T, norms


def solution(mesh):
    n_x, n_y = 2, 8
    geometry = (mesh.shape["dp"], mesh.shape["ctx"] // (n_x * n_y), n_x, n_y)
    placed = (P(("dp", "ctx"), None), P(("dp", "ctx"), None), P("dp", None), P("dp"), P("dp", None))
    return jax.shard_map(
        functools.partial(on_device, geometry),
        mesh=mesh,
        in_specs=placed,
        out_specs=(P(("dp", "ctx"), None), P("dp", None)),
        check_vma=False,
    )
```

```python
import functools

import jax
import jax.numpy as jnp
from jax import lax
from jax.experimental import pallas as pl
from jax.experimental.pallas import tpu as pltpu
from jax.sharding import PartitionSpec as P

CLIP_NORM = 128.0
LONGEST = 1536.0
LOCAL_DOCS = 23
REACH = 3
PARTS = 4
STRIP = 512
MESH = pl.DeviceIdType.MESH
F32 = jnp.float32
BF16 = jnp.bfloat16


def lane_tiles(array):
    return [array[:, k : k + 128] for k in range(0, array.shape[1], 128)]


def kernel(
    geometry, grad_hbm, inner_hbm, len_hbm, off_ref, inc_hbm,
    out_ref, norm_ref,
    grad, inner_ref, len_ref, inc_ref, lhs, last_out, first_out, last_in, first_in, last_far, first_far,
    terms_out, terms_in, clipped, send_1, recv_1, send_2, recv_2, send_3, recv_3,
    load_sem, small_sem, halo_send, halo_recv, terms_send, terms_recv,
    send_sem_1, recv_sem_1, send_sem_2, recv_sem_2, send_sem_3, recv_sem_3,
):
    n_dp, n_z, n_x, n_y = geometry
    n_ctx = n_z * n_x * n_y
    rows, width = grad.shape
    rank = inner_ref.shape[0]
    docs = len_ref.shape[1]
    part = width // PARTS
    tokens = n_ctx * rows
    dp = lax.axis_index("dp")
    block = lax.axis_index("ctx")
    z, x, y = block // (n_x * n_y), (block // n_y) % n_x, block % n_y
    n_group = n_dp * n_x
    group = dp * n_x + x

    def along(distance):
        return (dp, lax.rem(block + distance + n_ctx, n_ctx))

    def in_group(g):
        return (g // n_x, z * (n_x * n_y) + lax.rem(g, n_x) * n_y + y)

    def in_z(other):
        return (dp, other * (n_x * n_y) + x * n_y + y)

    def in_y(other):
        return (dp, z * (n_x * n_y) + x * n_y + other)

    smalls = []
    for i, (hbm, ref) in enumerate(
        ((len_hbm, len_ref), (inner_hbm, inner_ref), (inc_hbm, inc_ref))
    ):
        smalls.append(pltpu.make_async_copy(hbm, ref, small_sem.at[i]))
        smalls[-1].start()
    loads = []
    for p in range(PARTS):
        columns = pl.ds(p * part, part)
        loads.append(
            pltpu.make_async_copy(grad_hbm.at[:, columns], grad.at[:, columns], load_sem.at[p])
        )
        loads[-1].start()

    barrier = pltpu.get_barrier_semaphore()
    greeted = 0
    for distance in range(1, REACH + 1):
        for sign in (1, -1):
            pl.semaphore_signal(
                barrier, inc=1, device_id=along(sign * distance), device_id_type=MESH
            )
            greeted += 1
    for size, me, where in ((n_group, group, in_group), (n_z, z, in_z), (n_y, y, in_y)):
        for step in range(1, size):
            pl.semaphore_signal(
                barrier, inc=1, device_id=where(lax.rem(me + step, size)), device_id_type=MESH
            )
            greeted += 1

    for copy in smalls:
        copy.wait()
    lengths = len_ref[...].astype(F32)
    down = lax.broadcasted_iota(jnp.int32, (docs, docs), 0)
    across = lax.broadcasted_iota(jnp.int32, (docs, docs), 1)
    own = down == across
    spread = jnp.broadcast_to(lengths, (docs, docs))
    ends = jnp.sum(jnp.where(across <= down, spread, 0.0), axis=1, keepdims=True)
    length = jnp.sum(jnp.where(own, spread, 0.0), axis=1, keepdims=True)
    start = jnp.min(
        jnp.where(length == LONGEST, ends - length, float(tokens)), axis=0, keepdims=True
    )
    shift = start + off_ref[0].astype(F32)

    def ids_of(positions):
        packed = positions.astype(F32) + shift
        packed = jnp.where(packed >= tokens, packed - tokens, packed)
        return jnp.sum(jnp.where(ends <= packed, 1.0, 0.0), axis=0, keepdims=True)

    ids = ids_of(block * rows + lax.broadcasted_iota(jnp.int32, (1, rows), 1))
    lane = lax.broadcasted_iota(jnp.int32, (1, 128), 1)
    places = jnp.zeros((1, 128), jnp.int32)
    offsets = (-rows - 1, -1, 0, rows, 2 * rows, rows - 1)
    for i, offset in enumerate(offsets):
        places = jnp.where(lane == i, offset, places)
    places = places + block * rows
    places = jnp.where(places < 0, places + tokens, places)
    places = jnp.where(places >= tokens, places - tokens, places)
    edge_ids = ids_of(places)
    behind_2, behind_1, first, ahead_1, ahead_2, last = [
        jnp.sum(jnp.where(lane == i, edge_ids, 0.0), axis=1, keepdims=True)
        for i in range(len(offsets))
    ]

    inner = inner_ref[...].astype(F32)
    local = ids - first
    local = jnp.where(local < 0.0, local + docs, local)
    lhs[0:rank, :] = jnp.where(ids == last, inner, 0.0).astype(BF16)

    def select_docs(begin, end):
        for q in range(begin, end):
            lhs[(q + 1) * rank : (q + 2) * rank, :] = jnp.where(
                local == float(q), inner, 0.0
            ).astype(BF16)

    select_docs(0, 1)

    def halo(p):
        columns = pl.ds(p * part, part)
        far = pl.ds((p % (PARTS // 2)) * part, part)
        low = p < PARTS // 2
        moves = [
            (last_out.at[:, columns], last_in.at[:, columns], along(1)),
            (first_out.at[:, columns], first_in.at[:, columns], along(-1)),
            (last_out.at[:, columns], last_far.at[:, far], along(2))
            if low
            else (first_out.at[:, columns], first_far.at[:, far], along(-2)),
        ]
        return [
            pltpu.make_async_remote_copy(
                src_ref=src,
                dst_ref=dst,
                send_sem=halo_send.at[p, i],
                recv_sem=halo_recv.at[p, i],
                device_id=to,
                device_id_type=MESH,
            )
            for i, (src, dst, to) in enumerate(moves)
        ]

    doc_rows = LOCAL_DOCS * rank
    squares_first = jnp.zeros((rank, 128), F32)
    halos = []
    for p in range(PARTS):
        loads[p].wait()
        columns = slice(p * part, (p + 1) * part)
        sums = jnp.dot(lhs[0 : 2 * rank, :], grad[:, columns], preferred_element_type=F32)
        last_out[:, columns] = sums[0:rank].astype(BF16)
        first_out[:, columns] = sums[rank : 2 * rank].astype(BF16)
        if p == 0:
            pl.semaphore_wait(barrier, greeted)
        halos.append(halo(p))
        for copy in reversed(halos[-1]):
            copy.start()
        for tile in lane_tiles(sums[rank : 2 * rank]):
            squares_first = squares_first + tile * tile
    select_docs(1, LOCAL_DOCS)

    def add_squares(i, squares):
        columns = pl.ds(pl.multiple_of(i * STRIP, 128), STRIP)
        sums = jnp.dot(lhs[2 * rank :, :], grad[:, columns], preferred_element_type=F32)
        for tile in lane_tiles(sums):
            squares = squares + tile * tile
        return squares

    squares = jnp.zeros((doc_rows - rank, 128), F32)
    squares = lax.fori_loop(0, width // STRIP, add_squares, squares)
    squares = jnp.concatenate([squares_first, squares], axis=0)

    by_row = jnp.sum(squares, axis=1, keepdims=True)
    label = first + lax.shift_right_logical(
        lax.broadcasted_iota(jnp.int32, (doc_rows, 1), 0), rank.bit_length() - 1
    ).astype(F32)
    label = jnp.where(label >= docs, label - docs, label)
    lane_f = lane.astype(F32)
    terms = jnp.sum(jnp.where(label == lane_f, by_row, 0.0), axis=0, keepdims=True)

    def flag(condition):
        return jnp.where(condition, 2.0, 0.0)

    pair_1 = flag(behind_1 == first)
    pair_2 = flag(behind_1 == ahead_1)
    pair_3_ahead = flag(behind_1 == ahead_2)
    pair_3_behind = flag(behind_2 == ahead_1)
    crossed = jnp.zeros((rank, 128), F32)
    for p in range(PARTS):
        columns = slice(p * part, (p + 1) * part)
        far = slice((p % (PARTS // 2)) * part, (p % (PARTS // 2) + 1) * part)
        for copy in halos[p]:
            copy.wait_recv()
        from_behind = last_in[:, columns].astype(F32)
        from_ahead = first_in[:, columns].astype(F32)
        partner = pair_1 * first_out[:, columns].astype(F32) + pair_2 * from_ahead
        if p < PARTS // 2:
            product = from_behind * partner + (pair_3_behind * from_ahead) * last_far[
                :, far
            ].astype(F32)
        else:
            product = from_behind * (partner + pair_3_ahead * first_far[:, far].astype(F32))
        for tile in lane_tiles(product):
            crossed = crossed + tile
    cross = jnp.sum(jnp.sum(crossed, axis=1, keepdims=True), axis=0, keepdims=True)
    terms = terms + jnp.where(lane_f == first, cross, 0.0)

    terms_out[...] = jnp.broadcast_to(terms, (8, 128))
    news = []
    for distance in range(1, REACH + 1):
        for sign in (1, -1):
            slot = len(news)
            news.append(
                pltpu.make_async_remote_copy(
                    src_ref=terms_out,
                    dst_ref=terms_in.at[slot],
                    send_sem=terms_send.at[slot],
                    recv_sem=terms_recv.at[slot],
                    device_id=along(sign * distance),
                    device_id_type=MESH,
                )
            )
            news[-1].start()
    near = terms
    for slot, copy in enumerate(news):
        copy.wait_recv()
        near = near + terms_in[slot, 0:1, :]
    for step in range(1, n_x):
        slot = len(news)
        news.append(
            pltpu.make_async_remote_copy(
                src_ref=terms_out,
                dst_ref=terms_in.at[slot],
                send_sem=terms_send.at[slot],
                recv_sem=terms_recv.at[slot],
                device_id=in_group(dp * n_x + lax.rem(x + step, n_x)),
                device_id_type=MESH,
            )
        )
        news[-1].start()

    norms = jnp.sqrt(jnp.maximum(near[:, 0:docs], 0.0))
    factor = inc_ref[...].astype(F32) * CLIP_NORM / jnp.maximum(norms, CLIP_NORM)
    factor = jnp.sum(jnp.where(own, jnp.broadcast_to(factor, (docs, docs)), 0.0), axis=1, keepdims=True)
    name = lax.broadcasted_iota(jnp.int32, (docs, 1), 0).astype(F32)
    token_factor = jnp.sum(jnp.where(ids == name, factor, 0.0), axis=0, keepdims=True)
    scaled = (token_factor * inner).astype(BF16)

    each = width // (n_dp * n_ctx)
    run = n_y * each
    slab = n_z * run

    def share(step, offset):
        slot = (step - 1) * n_x + offset - 1
        to = lax.rem(dp + step, n_dp) * n_x + lax.rem(x + offset, n_x)
        return pltpu.make_async_remote_copy(
            src_ref=send_1.at[slot],
            dst_ref=recv_1.at[slot],
            send_sem=send_sem_1.at[slot],
            recv_sem=recv_sem_1.at[slot],
            device_id=in_group(to),
            device_id_type=MESH,
        )

    def multiply(step, offsets):
        to_dp = lax.rem(dp + step, n_dp)
        columns = pl.ds(pl.multiple_of(to_dp * (n_x * slab), 128), n_x * slab)
        sums = jnp.dot(scaled, grad[:, columns], preferred_element_type=F32)
        for other in range(n_x):
            for k in range(n_z):
                column = (k * n_x + other) * run
                clipped[other, :, k * run : (k + 1) * run] = sums[:, column : column + run]
        for offset in offsets:
            slot = (step - 1) * n_x + offset - 1
            send_1[slot] = clipped[lax.rem(x + offset, n_x)].astype(BF16)
            share(step, offset).start()

    @pl.loop(1, n_dp)
    def _(step):
        multiply(step, range(1, n_x + 1))

    multiply(n_dp, range(1, n_x))
    sent = [
        share(step, offset)
        for step in range(1, n_dp + 1)
        for offset in range(1, n_x + 1)
        if (step, offset) != (n_dp, n_x)
    ]

    def exchange(size, me, where, out, into, out_sem, in_sem):
        copies = []
        for step in range(1, size):
            to = lax.rem(me + step, size)
            copies.append(
                pltpu.make_async_remote_copy(
                    src_ref=out.at[to],
                    dst_ref=into.at[me],
                    send_sem=out_sem.at[step],
                    recv_sem=in_sem.at[me],
                    device_id=where(to),
                    device_id_type=MESH,
                )
            )
            copies[-1].start()
        into[me] = out[me]
        for step in range(1, size):
            source = lax.rem(me + size - step, size)
            pltpu.make_async_remote_copy(
                src_ref=out.at[source],
                dst_ref=into.at[source],
                send_sem=out_sem.at[step],
                recv_sem=in_sem.at[source],
                device_id=where(source),
                device_id_type=MESH,
            ).wait_recv()
        return copies

    all_terms = terms
    for slot in range(2 * REACH, len(news)):
        news[slot].wait_recv()
        all_terms = all_terms + terms_in[slot, 0:1, :]
    total = clipped[x, :, 0:slab]
    for slot, copy in enumerate(sent):
        copy.wait_recv()
        total = total + recv_1[slot, :, 0:slab].astype(F32)
    wide = send_2.shape[2]
    for k in range(n_z):
        send_2[k, :, 0:run] = total[0:8, k * run : (k + 1) * run]
        send_2[k, :, run : 2 * run] = total[8:16, k * run : (k + 1) * run]
        send_2[k, :, wide - docs :] = jnp.broadcast_to(all_terms[:, 0:docs], (8, docs))
    sent += exchange(n_z, z, in_z, send_2, recv_2, send_sem_2, recv_sem_2)
    received = recv_2[0]
    for k in range(1, n_z):
        received = received + recv_2[k]
    for k in range(n_y):
        send_3[k, :, 0:each] = received[:, k * each : (k + 1) * each]
        send_3[k, :, each : 2 * each] = received[:, run + k * each : run + (k + 1) * each]
        send_3[k, :, send_3.shape[2] - docs :] = received[:, wide - docs :]
    sent += exchange(n_y, y, in_y, send_3, recv_3, send_sem_3, recv_sem_3)
    received = recv_3[0]
    for k in range(1, n_y):
        received = received + recv_3[k]
    out_ref[0:8, :] = received[:, 0:each]
    out_ref[8:16, :] = received[:, each : 2 * each]
    norm_ref[...] = jnp.sqrt(jnp.maximum(received[0:1, send_3.shape[2] - docs :], 0.0))

    for copies in halos:
        for copy in copies:
            copy.wait_send()
    for copy in news + sent:
        copy.wait_send()


def on_device(geometry, out_grad, adapter_inner, doc_lengths, slab_offset, included):
    n_dp, n_z, n_x, n_y = geometry
    n_group = n_dp * n_x
    rows, width = out_grad.shape
    rank = adapter_inner.shape[1]
    docs = doc_lengths.shape[1]
    each = width // (n_dp * n_z * n_x * n_y)
    depth = (LOCAL_DOCS + 1) * rank
    long = pl.cdiv(n_z * n_y * each, 128) * 128
    short = pl.cdiv(2 * each + docs, 128) * 128
    wide = pl.cdiv(2 * n_y * each + docs, 128) * 128
    in_vmem = pl.BlockSpec(memory_space=pltpu.VMEM)
    in_hbm = pl.BlockSpec(memory_space=pltpu.HBM)
    dma = pltpu.SemaphoreType.DMA
    gradient, norms = pl.pallas_call(
        functools.partial(kernel, geometry),
        out_shape=(
            jax.ShapeDtypeStruct((rank, each), F32),
            jax.ShapeDtypeStruct((1, docs), F32),
        ),
        in_specs=[
            in_hbm,
            in_hbm,
            in_hbm,
            pl.BlockSpec(memory_space=pltpu.SMEM),
            in_hbm,
        ],
        out_specs=(in_vmem, in_vmem),
        scratch_shapes=[
            pltpu.VMEM((rows, width), BF16),
            pltpu.VMEM((rank, rows), BF16),
            pltpu.VMEM((1, docs), jnp.int32),
            pltpu.VMEM((1, docs), jnp.int32),
            pltpu.VMEM((depth, rows), BF16),
            pltpu.VMEM((rank, width), BF16),
            pltpu.VMEM((rank, width), BF16),
            pltpu.VMEM((rank, width), BF16),
            pltpu.VMEM((rank, width), BF16),
            pltpu.VMEM((rank, width // 2), BF16),
            pltpu.VMEM((rank, width // 2), BF16),
            pltpu.VMEM((8, 128), F32),
            pltpu.VMEM((2 * REACH + n_x - 1, 8, 128), F32),
            pltpu.VMEM((n_x, rank, long), F32),
            pltpu.VMEM((n_group - 1, rank, long), BF16),
            pltpu.VMEM((n_group - 1, rank, long), BF16),
            pltpu.VMEM((n_z, 8, wide), F32),
            pltpu.VMEM((n_z, 8, wide), F32),
            pltpu.VMEM((n_y, 8, short), F32),
            pltpu.VMEM((n_y, 8, short), F32),
            dma((PARTS,)),
            dma((3,)),
            dma((PARTS, 3)),
            dma((PARTS, 3)),
            dma((2 * REACH + n_x - 1,)),
            dma((2 * REACH + n_x - 1,)),
            dma((n_group - 1,)),
            dma((n_group - 1,)),
            dma((n_z,)),
            dma((n_z,)),
            dma((n_y,)),
            dma((n_y,)),
        ],
        compiler_params=pltpu.CompilerParams(
            collective_id=0, has_side_effects=True, vmem_limit_bytes=60 * 2**20
        ),
    )(out_grad, adapter_inner.T, doc_lengths, slab_offset, included)
    return gradient.T, norms


def solution(mesh):
    n_x, n_y = 2, 8
    geometry = (mesh.shape["dp"], mesh.shape["ctx"] // (n_x * n_y), n_x, n_y)
    placed = (P(("dp", "ctx"), None), P(("dp", "ctx"), None), P("dp", None), P("dp"), P("dp", None))
    return jax.shard_map(
        functools.partial(on_device, geometry),
        mesh=mesh,
        in_specs=placed,
        out_specs=(P(("dp", "ctx"), None), P("dp", None)),
        check_vma=False,
    )
```

```python
import functools

import jax
import jax.numpy as jnp
from jax import lax
from jax.experimental import pallas as pl
from jax.experimental.pallas import tpu as pltpu
from jax.sharding import PartitionSpec as P

CLIP_NORM = 128.0
LONGEST = 1536.0
LOCAL_DOCS = 23
REACH = 3
PARTS = 4
STRIP = 512
MESH = pl.DeviceIdType.MESH
F32 = jnp.float32
BF16 = jnp.bfloat16


def lane_tiles(array):
    return [array[:, k : k + 128] for k in range(0, array.shape[1], 128)]


def kernel(
    geometry, grad_hbm, inner_hbm, len_hbm, off_ref, inc_hbm,
    out_ref, norm_ref,
    grad, inner_ref, len_ref, inc_ref, lhs, last_out, first_out, last_in, first_in, last_far, first_far,
    terms_out, terms_in, clipped, send_1, recv_1, send_2, recv_2, send_3, recv_3,
    load_sem, small_sem, halo_send, halo_recv, terms_send, terms_recv,
    send_sem_1, recv_sem_1, send_sem_2, recv_sem_2, send_sem_3, recv_sem_3,
):
    n_dp, n_z, n_x, n_y = geometry
    n_ctx = n_z * n_x * n_y
    rows, width = grad.shape
    rank = inner_ref.shape[0]
    docs = len_ref.shape[1]
    part = width // PARTS
    tokens = n_ctx * rows
    dp = lax.axis_index("dp")
    block = lax.axis_index("ctx")
    z, x, y = block // (n_x * n_y), (block // n_y) % n_x, block % n_y
    n_group = n_dp * n_x
    group = dp * n_x + x

    def along(distance):
        return (dp, lax.rem(block + distance + n_ctx, n_ctx))

    def in_group(g):
        return (g // n_x, z * (n_x * n_y) + lax.rem(g, n_x) * n_y + y)

    def in_z(other):
        return (dp, other * (n_x * n_y) + x * n_y + y)

    def in_y(other):
        return (dp, z * (n_x * n_y) + x * n_y + other)

    smalls = []
    for i, (hbm, ref) in enumerate(
        ((len_hbm, len_ref), (inner_hbm, inner_ref), (inc_hbm, inc_ref))
    ):
        smalls.append(pltpu.make_async_copy(hbm, ref, small_sem.at[i]))
        smalls[-1].start()
    loads = []
    for p in range(PARTS):
        columns = pl.ds(p * part, part)
        loads.append(
            pltpu.make_async_copy(grad_hbm.at[:, columns], grad.at[:, columns], load_sem.at[p])
        )
        loads[-1].start()

    barrier = pltpu.get_barrier_semaphore()
    greeted = 0
    for distance in range(1, REACH + 1):
        for sign in (1, -1):
            pl.semaphore_signal(
                barrier, inc=1, device_id=along(sign * distance), device_id_type=MESH
            )
            greeted += 1
    for size, me, where in ((n_group, group, in_group), (n_z, z, in_z), (n_y, y, in_y)):
        for step in range(1, size):
            pl.semaphore_signal(
                barrier, inc=1, device_id=where(lax.rem(me + step, size)), device_id_type=MESH
            )
            greeted += 1

    for copy in smalls:
        copy.wait()
    lengths = len_ref[...].astype(F32)
    down = lax.broadcasted_iota(jnp.int32, (docs, docs), 0)
    across = lax.broadcasted_iota(jnp.int32, (docs, docs), 1)
    own = down == across
    spread = jnp.broadcast_to(lengths, (docs, docs))
    ends = jnp.sum(jnp.where(across <= down, spread, 0.0), axis=1, keepdims=True)
    length = jnp.sum(jnp.where(own, spread, 0.0), axis=1, keepdims=True)
    start = jnp.min(
        jnp.where(length == LONGEST, ends - length, float(tokens)), axis=0, keepdims=True
    )
    shift = start + off_ref[0].astype(F32)

    def ids_of(positions):
        packed = positions.astype(F32) + shift
        packed = jnp.where(packed >= tokens, packed - tokens, packed)
        return jnp.sum(jnp.where(ends <= packed, 1.0, 0.0), axis=0, keepdims=True)

    ids = ids_of(block * rows + lax.broadcasted_iota(jnp.int32, (1, rows), 1))
    lane = lax.broadcasted_iota(jnp.int32, (1, 128), 1)
    places = jnp.zeros((1, 128), jnp.int32)
    offsets = (-rows - 1, -1, 0, rows, 2 * rows, rows - 1)
    for i, offset in enumerate(offsets):
        places = jnp.where(lane == i, offset, places)
    places = places + block * rows
    places = jnp.where(places < 0, places + tokens, places)
    places = jnp.where(places >= tokens, places - tokens, places)
    edge_ids = ids_of(places)
    behind_2, behind_1, first, ahead_1, ahead_2, last = [
        jnp.sum(jnp.where(lane == i, edge_ids, 0.0), axis=1, keepdims=True)
        for i in range(len(offsets))
    ]

    inner = inner_ref[...].astype(F32)
    local = ids - first
    local = jnp.where(local < 0.0, local + docs, local)
    lhs[0:rank, :] = jnp.where(ids == last, inner, 0.0).astype(BF16)

    def select_docs(begin, end):
        for q in range(begin, end):
            lhs[(q + 1) * rank : (q + 2) * rank, :] = jnp.where(
                local == float(q), inner, 0.0
            ).astype(BF16)

    select_docs(0, 1)

    def halo(p):
        columns = pl.ds(p * part, part)
        far = pl.ds((p % (PARTS // 2)) * part, part)
        low = p < PARTS // 2
        moves = [
            (last_out.at[:, columns], last_in.at[:, columns], along(1)),
            (first_out.at[:, columns], first_in.at[:, columns], along(-1)),
            (last_out.at[:, columns], last_far.at[:, far], along(2))
            if low
            else (first_out.at[:, columns], first_far.at[:, far], along(-2)),
        ]
        return [
            pltpu.make_async_remote_copy(
                src_ref=src,
                dst_ref=dst,
                send_sem=halo_send.at[p, i],
                recv_sem=halo_recv.at[p, i],
                device_id=to,
                device_id_type=MESH,
            )
            for i, (src, dst, to) in enumerate(moves)
        ]

    doc_rows = LOCAL_DOCS * rank
    squares_first = jnp.zeros((rank, 128), F32)
    halos = []
    for p in range(PARTS):
        loads[p].wait()
        columns = slice(p * part, (p + 1) * part)
        sums = jnp.dot(lhs[0 : 2 * rank, :], grad[:, columns], preferred_element_type=F32)
        last_out[:, columns] = sums[0:rank].astype(BF16)
        first_out[:, columns] = sums[rank : 2 * rank].astype(BF16)
        if p == 0:
            pl.semaphore_wait(barrier, greeted)
        halos.append(halo(p))
        for copy in reversed(halos[-1]):
            copy.start()
        for tile in lane_tiles(sums[rank : 2 * rank]):
            squares_first = squares_first + tile * tile
    select_docs(1, LOCAL_DOCS)

    def add_squares(i, squares):
        columns = pl.ds(pl.multiple_of(i * STRIP, 128), STRIP)
        sums = jnp.dot(lhs[2 * rank :, :], grad[:, columns], preferred_element_type=F32)
        for tile in lane_tiles(sums):
            squares = squares + tile * tile
        return squares

    squares = jnp.zeros((doc_rows - rank, 128), F32)
    squares = lax.fori_loop(0, width // STRIP, add_squares, squares)
    squares = jnp.concatenate([squares_first, squares], axis=0)

    by_row = jnp.sum(squares, axis=1, keepdims=True)
    label = first + lax.shift_right_logical(
        lax.broadcasted_iota(jnp.int32, (doc_rows, 1), 0), rank.bit_length() - 1
    ).astype(F32)
    label = jnp.where(label >= docs, label - docs, label)
    lane_f = lane.astype(F32)
    terms = jnp.sum(jnp.where(label == lane_f, by_row, 0.0), axis=0, keepdims=True)

    def flag(condition):
        return jnp.where(condition, 2.0, 0.0)

    pair_1 = flag(behind_1 == first)
    pair_2 = flag(behind_1 == ahead_1)
    pair_3_ahead = flag(behind_1 == ahead_2)
    pair_3_behind = flag(behind_2 == ahead_1)
    crossed = jnp.zeros((rank, 128), F32)
    for p in range(PARTS):
        columns = slice(p * part, (p + 1) * part)
        far = slice((p % (PARTS // 2)) * part, (p % (PARTS // 2) + 1) * part)
        for copy in halos[p]:
            copy.wait_recv()
        from_behind = last_in[:, columns].astype(F32)
        from_ahead = first_in[:, columns].astype(F32)
        partner = pair_1 * first_out[:, columns].astype(F32) + pair_2 * from_ahead
        if p < PARTS // 2:
            product = from_behind * partner + (pair_3_behind * from_ahead) * last_far[
                :, far
            ].astype(F32)
        else:
            product = from_behind * (partner + pair_3_ahead * first_far[:, far].astype(F32))
        for tile in lane_tiles(product):
            crossed = crossed + tile
    cross = jnp.sum(jnp.sum(crossed, axis=1, keepdims=True), axis=0, keepdims=True)
    terms = terms + jnp.where(lane_f == first, cross, 0.0)

    terms_out[...] = jnp.broadcast_to(terms, (8, 128))
    news = []
    for distance in range(REACH, 0, -1):
        for sign in (1, -1):
            slot = len(news)
            news.append(
                pltpu.make_async_remote_copy(
                    src_ref=terms_out,
                    dst_ref=terms_in.at[slot],
                    send_sem=terms_send.at[slot],
                    recv_sem=terms_recv.at[slot],
                    device_id=along(sign * distance),
                    device_id_type=MESH,
                )
            )
            news[-1].start()
    near = terms
    for slot, copy in enumerate(news):
        copy.wait_recv()
        near = near + terms_in[slot, 0:1, :]
    for step in range(1, n_x):
        slot = len(news)
        news.append(
            pltpu.make_async_remote_copy(
                src_ref=terms_out,
                dst_ref=terms_in.at[slot],
                send_sem=terms_send.at[slot],
                recv_sem=terms_recv.at[slot],
                device_id=in_group(dp * n_x + lax.rem(x + step, n_x)),
                device_id_type=MESH,
            )
        )
        news[-1].start()

    norms = jnp.sqrt(jnp.maximum(near[:, 0:docs], 0.0))
    factor = inc_ref[...].astype(F32) * CLIP_NORM / jnp.maximum(norms, CLIP_NORM)
    factor = jnp.sum(jnp.where(own, jnp.broadcast_to(factor, (docs, docs)), 0.0), axis=1, keepdims=True)
    name = lax.broadcasted_iota(jnp.int32, (docs, 1), 0).astype(F32)
    token_factor = jnp.sum(jnp.where(ids == name, factor, 0.0), axis=0, keepdims=True)
    scaled = (token_factor * inner).astype(BF16)

    each = width // (n_dp * n_ctx)
    run = n_y * each
    slab = n_z * run

    def share(step, offset):
        slot = (step - 1) * n_x + offset - 1
        to = lax.rem(dp + step, n_dp) * n_x + lax.rem(x + offset, n_x)
        return pltpu.make_async_remote_copy(
            src_ref=send_1.at[slot],
            dst_ref=recv_1.at[slot],
            send_sem=send_sem_1.at[slot],
            recv_sem=recv_sem_1.at[slot],
            device_id=in_group(to),
            device_id_type=MESH,
        )

    def multiply(step, offsets):
        to_dp = lax.rem(dp + step, n_dp)
        columns = pl.ds(pl.multiple_of(to_dp * (n_x * slab), 128), n_x * slab)
        sums = jnp.dot(scaled, grad[:, columns], preferred_element_type=F32)
        for other in range(n_x):
            for k in range(n_z):
                column = (k * n_x + other) * run
                clipped[other, :, k * run : (k + 1) * run] = sums[:, column : column + run]
        for offset in offsets:
            slot = (step - 1) * n_x + offset - 1
            send_1[slot] = clipped[lax.rem(x + offset, n_x)].astype(BF16)
            share(step, offset).start()

    @pl.loop(1, n_dp)
    def _(step):
        multiply(step, range(1, n_x + 1))

    multiply(n_dp, range(1, n_x))
    sent = [
        share(step, offset)
        for step in range(1, n_dp + 1)
        for offset in range(1, n_x + 1)
        if (step, offset) != (n_dp, n_x)
    ]

    def exchange(size, me, where, out, into, out_sem, in_sem):
        copies = []
        for step in sorted(range(1, size), key=lambda k: -min(k, size - k)):
            to = lax.rem(me + step, size)
            copies.append(
                pltpu.make_async_remote_copy(
                    src_ref=out.at[to],
                    dst_ref=into.at[me],
                    send_sem=out_sem.at[step],
                    recv_sem=in_sem.at[me],
                    device_id=where(to),
                    device_id_type=MESH,
                )
            )
            copies[-1].start()
        into[me] = out[me]
        for step in range(1, size):
            source = lax.rem(me + size - step, size)
            pltpu.make_async_remote_copy(
                src_ref=out.at[source],
                dst_ref=into.at[source],
                send_sem=out_sem.at[step],
                recv_sem=in_sem.at[source],
                device_id=where(source),
                device_id_type=MESH,
            ).wait_recv()
        return copies

    all_terms = terms
    for slot in range(2 * REACH, len(news)):
        news[slot].wait_recv()
        all_terms = all_terms + terms_in[slot, 0:1, :]
    total = clipped[x, :, 0:slab]
    for slot, copy in enumerate(sent):
        copy.wait_recv()
        total = total + recv_1[slot, :, 0:slab].astype(F32)
    wide = send_2.shape[2]
    for k in range(n_z):
        send_2[k, :, 0:run] = total[0:8, k * run : (k + 1) * run]
        send_2[k, :, run : 2 * run] = total[8:16, k * run : (k + 1) * run]
        send_2[k, :, wide - docs :] = jnp.broadcast_to(all_terms[:, 0:docs], (8, docs))
    sent += exchange(n_z, z, in_z, send_2, recv_2, send_sem_2, recv_sem_2)
    received = recv_2[0]
    for k in range(1, n_z):
        received = received + recv_2[k]
    for k in range(n_y):
        send_3[k, :, 0:each] = received[:, k * each : (k + 1) * each]
        send_3[k, :, each : 2 * each] = received[:, run + k * each : run + (k + 1) * each]
        send_3[k, :, send_3.shape[2] - docs :] = received[:, wide - docs :]
    sent += exchange(n_y, y, in_y, send_3, recv_3, send_sem_3, recv_sem_3)
    received = recv_3[0]
    for k in range(1, n_y):
        received = received + recv_3[k]
    out_ref[0:8, :] = received[:, 0:each]
    out_ref[8:16, :] = received[:, each : 2 * each]
    norm_ref[...] = jnp.sqrt(jnp.maximum(received[0:1, send_3.shape[2] - docs :], 0.0))

    for copies in halos:
        for copy in copies:
            copy.wait_send()
    for copy in news + sent:
        copy.wait_send()


def on_device(geometry, out_grad, adapter_inner, doc_lengths, slab_offset, included):
    n_dp, n_z, n_x, n_y = geometry
    n_group = n_dp * n_x
    rows, width = out_grad.shape
    rank = adapter_inner.shape[1]
    docs = doc_lengths.shape[1]
    each = width // (n_dp * n_z * n_x * n_y)
    depth = (LOCAL_DOCS + 1) * rank
    long = pl.cdiv(n_z * n_y * each, 128) * 128
    short = pl.cdiv(2 * each + docs, 128) * 128
    wide = pl.cdiv(2 * n_y * each + docs, 128) * 128
    in_vmem = pl.BlockSpec(memory_space=pltpu.VMEM)
    in_hbm = pl.BlockSpec(memory_space=pltpu.HBM)
    dma = pltpu.SemaphoreType.DMA
    gradient, norms = pl.pallas_call(
        functools.partial(kernel, geometry),
        out_shape=(
            jax.ShapeDtypeStruct((rank, each), F32),
            jax.ShapeDtypeStruct((1, docs), F32),
        ),
        in_specs=[
            in_hbm,
            in_hbm,
            in_hbm,
            pl.BlockSpec(memory_space=pltpu.SMEM),
            in_hbm,
        ],
        out_specs=(in_vmem, in_vmem),
        scratch_shapes=[
            pltpu.VMEM((rows, width), BF16),
            pltpu.VMEM((rank, rows), BF16),
            pltpu.VMEM((1, docs), jnp.int32),
            pltpu.VMEM((1, docs), jnp.int32),
            pltpu.VMEM((depth, rows), BF16),
            pltpu.VMEM((rank, width), BF16),
            pltpu.VMEM((rank, width), BF16),
            pltpu.VMEM((rank, width), BF16),
            pltpu.VMEM((rank, width), BF16),
            pltpu.VMEM((rank, width // 2), BF16),
            pltpu.VMEM((rank, width // 2), BF16),
            pltpu.VMEM((8, 128), F32),
            pltpu.VMEM((2 * REACH + n_x - 1, 8, 128), F32),
            pltpu.VMEM((n_x, rank, long), F32),
            pltpu.VMEM((n_group - 1, rank, long), BF16),
            pltpu.VMEM((n_group - 1, rank, long), BF16),
            pltpu.VMEM((n_z, 8, wide), F32),
            pltpu.VMEM((n_z, 8, wide), F32),
            pltpu.VMEM((n_y, 8, short), F32),
            pltpu.VMEM((n_y, 8, short), F32),
            dma((PARTS,)),
            dma((3,)),
            dma((PARTS, 3)),
            dma((PARTS, 3)),
            dma((2 * REACH + n_x - 1,)),
            dma((2 * REACH + n_x - 1,)),
            dma((n_group - 1,)),
            dma((n_group - 1,)),
            dma((n_z,)),
            dma((n_z,)),
            dma((n_y,)),
            dma((n_y,)),
        ],
        compiler_params=pltpu.CompilerParams(
            collective_id=0, has_side_effects=True, vmem_limit_bytes=60 * 2**20
        ),
    )(out_grad, adapter_inner.T, doc_lengths, slab_offset, included)
    return gradient.T, norms


def solution(mesh):
    n_x, n_y = 2, 8
    geometry = (mesh.shape["dp"], mesh.shape["ctx"] // (n_x * n_y), n_x, n_y)
    placed = (P(("dp", "ctx"), None), P(("dp", "ctx"), None), P("dp", None), P("dp"), P("dp", None))
    return jax.shard_map(
        functools.partial(on_device, geometry),
        mesh=mesh,
        in_specs=placed,
        out_specs=(P(("dp", "ctx"), None), P("dp", None)),
        check_vma=False,
    )
```
